32 devices in a mesh: dp: 8 (over z, x), mp: 4 (over y, core).
Axes of the slice: x: 2, y: 2, z: 4, core: 2. Of those that a mesh axis runs over, the one named last changes fastest.
Arguments:
- owner: int32 [16384, 1], P(('dp', 'mp')), may hold values from 0 to 7; in each aligned block of 512 rows (0 to 511, 512 to 1023, ...) at most 256 rows name the same one
- slot: int32 [16384], P(('dp', 'mp')), may hold values from 0 to 8191
- table: bfloat16 [65536, 512], P('dp'), may hold values from -6 to 6
- w_in1: bfloat16 [512, 8, 256], P(None, None, 'mp'), may hold values from -0.25 to 0.25
- b_in1: bfloat16 [8, 256], P(None, 'mp'), may hold values from -4 to 4
- w_out1: bfloat16 [8, 256, 256], P(None, 'mp'), may hold values from -0.375 to 0.375
- b_out1: bfloat16 [8, 256], replicated, may hold values from -0.75 to 0.75
- gate1: bfloat16 [512, 2, 8], replicated, may hold values from -0.125 to 0.125
- w_in2: bfloat16 [512, 8, 256], P(None, None, 'mp'), may hold values from -0.25 to 0.25
- b_in2: bfloat16 [8, 256], P(None, 'mp'), may hold values from -4 to 4
- w_out2: bfloat16 [8, 256, 256], P(None, 'mp'), may hold values from -0.375 to 0.375
- b_out2: bfloat16 [8, 256], replicated, may hold values from -0.75 to 0.75
- gate2: bfloat16 [512, 3, 8], replicated, may hold values from -0.25 to 0.25
- tower_in: bfloat16 [3, 256, 128], replicated, may hold values from -0.375 to 0.375
- tower_bias: bfloat16 [3, 128], replicated, may hold values from -4 to 4
- tower_out: bfloat16 [3, 128], replicated, may hold values from -0.5 to 0.5
- tower_out_bias: bfloat16 [3], replicated, may hold values from -4 to 4
- pred_cot: float32 [3, 16384], P(None, ('dp', 'mp')), may hold values from -6 to 6
Outputs:
- predictions: float32 [3, 16384], P(None, ('dp', 'mp'))
- table_grad: float32 [65536, 512], P('dp', 'mp')
- w_in1_grad: float32 [512, 8, 256], P(None, None, 'mp')
- b_in1_grad: float32 [8, 256], P(None, 'mp')
- w_out1_grad: float32 [8, 256, 256], P(None, 'mp')
- b_out1_grad: float32 [8, 256], replicated
- gate1_grad: float32 [512, 2, 8], replicated
- w_in2_grad: float32 [512, 8, 256], P(None, None, 'mp')
- b_in2_grad: float32 [8, 256], P(None, 'mp')
- w_out2_grad: float32 [8, 256, 256], P(None, 'mp')
- b_out2_grad: float32 [8, 256], replicated
- gate2_grad: float32 [512, 3, 8], replicated
- tower_in_grad: float32 [3, 256, 128], replicated
- tower_bias_grad: float32 [3, 128], replicated
- tower_out_grad: float32 [3, 128], replicated
- tower_out_bias_grad: float32 [3], replicated
The draws below stay inside these ranges and needn't reach their ends.
Inputs may be any that keep to these rules, and one draw needn't show every extreme that they name: Among the 512 rows of one device no owner is named by more than 256 rows, and in some devices' rows one owner by exactly 256.
All inputs are finite; a program needn't handle non-finite values.
Results may differ from the reference program's by a relative error of at most 0.025.
Values may be sent and summed in bfloat16 or wider, within the bound.
A program may use at most 128 MiB of HBM per device.

```python
import math
import jax
import jax.numpy as jnp
import numpy as np
from jax import lax

EMB = 512
HID = 256
EOUT = 256
EXPERTS = 8
TASKS = 3
TOWER = 128
VOCAB = 65536
ROW_DEV = 512
ROWS = 16384
VOCAB_DEV = 8192
CAP = 256
N_DP = 8


def set_ends(drawn, key, least, largest):
    index_at = [jax.random.randint(jax.random.fold_in(key, axis), (), 0, length) for axis, length in enumerate(drawn.shape)]
    main_axis = drawn.shape.index(max(drawn.shape))
    beside = index_at[:main_axis] + [(index_at[main_axis] + 1) % drawn.shape[main_axis]] + index_at[main_axis + 1:]
    return drawn.at[tuple(index_at)].set(least).at[tuple(beside)].set(largest)


def levels(own_key, dims, shards, smallest, top_value):
    def one(axis_at, parts):
        draws = jax.random.uniform(jax.random.fold_in(jax.random.fold_in(own_key, 6), axis_at), (parts,), jnp.float32, smallest / len(shards), top_value / len(shards))
        return jnp.repeat(jnp.exp(draws), dims[axis_at] // parts).reshape((-1,) + (1,) * (len(dims) - axis_at - 1))

    level = one(*shards[0])
    for cut in shards[1:]:
        level = level * one(*cut)
    return level


def cumulative_ranks(number_of, lean):
    portions = [(1 << 20) // math.isqrt(grade ** lean) + 1 for grade in range(1, number_of + 1)]
    deviation = 1 + sum(portions) // (1 << 30)
    return np.cumsum(np.array([max(1, weight // deviation) for weight in portions]))


def ranked(own_key, shape, count, slope):
    table = cumulative_ranks(count, slope)
    pick = jax.random.randint(jax.random.fold_in(own_key, 1), shape, 0, int(table[count - 1]))
    standing = jnp.searchsorted(jnp.asarray(table, jnp.int32), pick, side="right")
    return jax.random.permutation(jax.random.fold_in(own_key, 2), count)[standing].astype(jnp.int32)


def assign_block(rng, own, number, rows, count, top, limit, skew):
    ranking = jax.random.permutation(rng, count)
    crowded, common = load_shares(count, rows * top, limit, skew, True), load_shares(count, rows * top, limit, skew, False)
    places = jnp.arange(count)

    def named(sizes, turn):
        used = int((sizes > 0).sum())
        fixed = max(1, used // 4)
        moved = fixed + (places - fixed + turn * (used - fixed)) % max(1, count - fixed)
        return jnp.zeros((count,), jnp.int32).at[ranking[jnp.where(places < fixed, places, moved)]].set(jnp.asarray(sizes, jnp.int32))

    sizes = jnp.where(number % 4 == 0, named(crowded, number // 4), named(common, number - number // 4 - 1))
    mixed = jax.random.permutation(jax.random.fold_in(own, 3), count)
    source_of, receiver = mixed[0:count // 2 * 2:2], mixed[1:count // 2 * 2:2]
    room = jnp.minimum(sizes[source_of] - 1, limit - sizes[receiver]) // 2
    room = jnp.where((source_of == ranking[0]) | (receiver == ranking[0]) | (sizes[receiver] == 0), 0, jnp.maximum(room, 0))
    moved = jax.random.randint(jax.random.fold_in(own, 4), (count // 2,), 0, 1 << 20) % (room + 1)
    sizes = sizes.at[source_of].add(-moved).at[receiver].add(moved)
    members = jnp.searchsorted(jnp.cumsum(sizes), jnp.arange(rows * top), side="right").astype(jnp.int32)
    listing = members.reshape(top, rows).T
    listing = listing[jax.random.permutation(jax.random.fold_in(own, 1), rows)]
    turn = jax.random.randint(jax.random.fold_in(own, 2), (rows, 1), 0, top)
    return jnp.take_along_axis(listing, (jnp.arange(top)[None, :] + turn) % top, axis=1)


def load_shares(number_of, total, most, skew, full):
    loads = [(1 << 20) // math.isqrt(grade ** skew) + 1 for grade in range(1, number_of + 1)]
    largest = most if full else min(most, max(-(-total // number_of), total * loads[0] // sum(loads)))
    least = 1 if total - largest >= number_of - 1 else 0
    given, surplus = [largest] + [least] * (number_of - 1), total - largest - least * (number_of - 1)
    while surplus > 0:
        free = [i for i in range(1, number_of) if given[i] < largest] or [i for i in range(1, number_of) if given[i] < most]
        whole, budget = sum([loads[i] for i in free]), surplus
        for i in free:
            more = min(most - given[i], max(1, budget * loads[i] // whole), surplus)
            given[i] = given[i] + more
            surplus = surplus - more
    return np.array(given)


def scatter_about(stream_key, dims, scale, bound, shards=(), held_as=jnp.bfloat16):
    values = scale * jax.random.normal(stream_key, dims, jnp.float32)
    if shards:
        values = values * levels(stream_key, dims, shards, -0.22, 0.18)
    return jnp.clip(values, -bound, bound).astype(held_as)


def setup_inputs(seed: int = 0) -> dict:
    streams_of = jax.random.split(jax.random.key(seed), 19)
    owner_keys = jax.random.split(jax.random.fold_in(streams_of[0], 1), ROWS // ROW_DEV)
    owner_turns = jax.random.permutation(jax.random.fold_in(streams_of[0], 3), ROWS // ROW_DEV)
    owner = jax.vmap(lambda own, number: assign_block(jax.random.fold_in(streams_of[0], 2), own, number, ROW_DEV, N_DP, 1, CAP, 2))(owner_keys, owner_turns).reshape((ROWS, 1))
    slot = set_ends(ranked(streams_of[1], (ROWS,), VOCAB_DEV, 2), jax.random.fold_in(streams_of[1], 3), 0, VOCAB_DEV - 1).astype(jnp.int32)
    table = scatter_about(streams_of[2], (VOCAB, EMB), 1.0, 6.0, ((0, 8),))
    w_in1 = scatter_about(streams_of[3], (EMB, EXPERTS, HID), EMB ** -0.5, 0.25, ((2, 4),))
    b_in1 = scatter_about(streams_of[4], (EXPERTS, HID), 0.3, 4.0, ((1, 4),))
    w_out1 = scatter_about(streams_of[5], (EXPERTS, HID, EOUT), HID ** -0.5, 0.375, ((1, 4),))
    b_out1 = scatter_about(streams_of[6], (EXPERTS, EOUT), 0.05, 0.75)
    gate1 = scatter_about(streams_of[7], (EMB, 2, EXPERTS), (4 * EMB) ** -0.5, 0.125)
    w_in2 = scatter_about(streams_of[8], (2 * EOUT, EXPERTS, HID), (2 * EOUT) ** -0.5, 0.25, ((2, 4),))
    b_in2 = scatter_about(streams_of[9], (EXPERTS, HID), 0.3, 4.0, ((1, 4),))
    w_out2 = scatter_about(streams_of[10], (EXPERTS, HID, EOUT), HID ** -0.5, 0.375, ((1, 4),))
    b_out2 = scatter_about(streams_of[11], (EXPERTS, EOUT), 0.05, 0.75)
    gate2 = scatter_about(streams_of[12], (2 * EOUT, TASKS, EXPERTS), (2 * EOUT) ** -0.5, 0.25)
    tower_in = scatter_about(streams_of[13], (TASKS, EOUT, TOWER), EOUT ** -0.5, 0.375)
    tower_bias = scatter_about(streams_of[14], (TASKS, TOWER), 0.3, 4.0)
    tower_out = scatter_about(streams_of[15], (TASKS, TOWER), TOWER ** -0.5, 0.5)
    tower_out_bias = scatter_about(streams_of[16], (TASKS,), 0.5, 4.0)
    pred_cot = scatter_about(streams_of[17], (TASKS, ROWS), 1.0, 6.0, ((1, 32),), jnp.float32)
    return dict(owner=owner, slot=slot, table=table, w_in1=w_in1, b_in1=b_in1, w_out1=w_out1, b_out1=b_out1, gate1=gate1, w_in2=w_in2, b_in2=b_in2, w_out2=w_out2, b_out2=b_out2, gate2=gate2, tower_in=tower_in, tower_bias=tower_bias, tower_out=tower_out, tower_out_bias=tower_out_bias, pred_cot=pred_cot)


@jax.custom_vjp
def low(v):
    return lax.optimization_barrier(v.astype(jnp.bfloat16)).astype(jnp.float32)

@jax.custom_vjp
def low_back(v):
    return v

def low_keep(v):
    return (low(v), None)

def low_pass(kept, grad):
    return (grad,)

def back_keep(v):
    return (v, None)

def back_low(kept, grad):
    return (low(grad),)
low.defvjp(low_keep, low_pass)
low_back.defvjp(back_keep, back_low)
HIGH = lax.Precision.HIGHEST

def mixture(inputs, w_in, b_in, w_out, b_out, gate):
    width = inputs.shape[1]
    tasks = gate.shape[1]
    pre = jnp.dot(inputs, w_in.reshape(width, -1), precision=HIGH) + b_in.reshape(-1)
    pre = low_back(pre)
    hidden = low(jax.nn.silu(pre)).reshape(inputs.shape[0], EXPERTS, HID)
    outputs = jnp.einsum('rek,ekd->red', hidden, w_out, precision=HIGH) + b_out
    outputs = low_back(outputs)
    logits = jnp.dot(inputs, gate.reshape(width, -1), precision=HIGH)
    logits = low_back(logits).reshape(inputs.shape[0], tasks, EXPERTS)
    weights = jax.nn.softmax(logits, axis=-1)
    return jnp.einsum('rte,red->rtd', weights, outputs, precision=HIGH)

def forward(table, w_in1, b_in1, w_out1, b_out1, gate1, w_in2, b_in2, w_out2, b_out2, gate2, tower_in, tower_bias, tower_out, tower_out_bias, ids):
    first = table[ids]
    mixed_one = mixture(first, w_in1, b_in1, w_out1, b_out1, gate1)
    second = low(jnp.concatenate([mixed_one[:, 0, :], mixed_one[:, 1, :]], axis=-1))
    mixed_two = mixture(second, w_in2, b_in2, w_out2, b_out2, gate2)
    rounded = low(mixed_two)
    act = jnp.einsum('rtd,tdk->rtk', rounded, tower_in, precision=HIGH) + tower_bias
    act = low_back(act)
    logit = lax.optimization_barrier(jnp.sum(jax.nn.silu(act) * tower_out, axis=-1)) + tower_out_bias
    return jax.nn.sigmoid(logit).T

def reference(owner, slot, table, w_in1, b_in1, w_out1, b_out1, gate1, w_in2, b_in2, w_out2, b_out2, gate2, tower_in, tower_bias, tower_out, tower_out_bias, pred_cot):
    ids = (owner[:, 0] * VOCAB_DEV + slot).astype(jnp.int32)
    params = [table, w_in1, b_in1, w_out1, b_out1, gate1, w_in2, b_in2, w_out2, b_out2, gate2, tower_in, tower_bias, tower_out, tower_out_bias]
    params = [p.astype(jnp.float32) for p in params]

    def wrapped(*values):
        return forward(*values, ids)
    predictions, pullback = jax.vjp(wrapped, *params)
    grads = pullback(pred_cot.astype(jnp.float32))
    return (predictions, grads[0], grads[1], grads[2], grads[3], grads[4], grads[5], grads[6], grads[7], grads[8], grads[9], grads[10], grads[11], grads[12], grads[13], grads[14])
```

```python
import functools

import jax
import jax.numpy as jnp
from jax import lax
from jax.experimental import pallas as pl
from jax.experimental.pallas import tpu as pltpu
from jax.sharding import PartitionSpec as P

F32, BF16 = jnp.float32, jnp.bfloat16
MESH = pl.DeviceIdType.MESH
MIB = 2**20
VMEM, ANY = pltpu.VMEM, pl.ANY
NN, NT, TN = ((1,), (0,)), ((1,), (1,)), ((0,), (0,))


def dot(a, b, dims=NN):
    return lax.dot_general(a, b, (dims, ((), ())), preferred_element_type=F32)


def remote(src, dst, send_sem, recv_sem, device):
    return pltpu.make_async_remote_copy(
        src_ref=src,
        dst_ref=dst,
        send_sem=send_sem,
        recv_sem=recv_sem,
        device_id=device,
        device_id_type=MESH,
    )


def greet(peers):
    barrier = pltpu.get_barrier_semaphore()
    for peer in peers:
        pl.semaphore_signal(barrier, inc=1, device_id=peer, device_id_type=MESH)
    pl.semaphore_wait(barrier, len(peers))


def partners(n_dp):
    d, p = lax.axis_index("dp"), lax.axis_index("mp")
    return d, p, p + 1 - 2 * (p % 2), (p + 2) % 4, d + 1 - 2 * (d % 2)


def fetch_kernel(
    n_dp, cap, owner, slot, cot, ws1, ws2, table,
    x_t, req, place_out, wa1, wa2,
    send, recv, idx_v, idx_s, stage, tab, xbuf,
    own_sem, ag_send, ag_recv, rq_send, rq_recv, idx_sem, tab_sem,
):
    d, p, p1, p2, d1 = partners(n_dp)
    rows = owner.shape[1]
    half = ws1.shape[0] // 2
    dx = d % 2
    blocks = table.shape[0] // stage.shape[1]
    step = stage.shape[1]

    def load(b):
        return pltpu.make_async_copy(
            table.at[pl.ds(b * step, step)], stage.at[b % 2], tab_sem.at[b % 2]
        )

    for b in range(min(2, blocks)):
        load(b).start()

    greet([((d + k) % n_dp, p) for k in range(1, n_dp)] + [(d, p1), (d, p2)])

    shards, wholes = (ws1, ws2), (wa1, wa2)
    own, core, across = [], [], []
    for layer in range(2):
        ws, wa = shards[layer], wholes[layer]
        own.append(pltpu.make_async_copy(ws, wa.at[p], own_sem.at[layer]))
        core.append(
            remote(ws, wa.at[p], ag_send.at[layer, 0], ag_recv.at[layer, 0], (d, p1))
        )
        mine = pl.ds(half * dx, half)
        across.append(
            remote(
                ws.at[mine], wa.at[p, mine], ag_send.at[layer, 1], ag_recv.at[layer, 1], (d, p2)
            )
        )
        across[layer].start()
        own[layer].start()
        core[layer].start()

    own_row = owner[...]
    count = max(8, n_dp)
    ks = lax.broadcasted_iota(jnp.int32, (count, rows), 0)
    onehot = jnp.where(ks == own_row, 1.0, 0.0)
    upper = jnp.where(
        lax.broadcasted_iota(jnp.int32, (rows, rows), 0)
        < lax.broadcasted_iota(jnp.int32, (rows, rows), 1),
        1.0,
        0.0,
    ).astype(BF16)
    before = dot(onehot.astype(BF16), upper)
    rank = jnp.sum(before * onehot, axis=0, keepdims=True).astype(jnp.int32)
    place = own_row * cap + rank
    place_out[...] = place
    slots = slot[...]
    c = cot[...]
    high = c.astype(BF16).astype(F32)
    mid = (c - high).astype(BF16).astype(F32)
    low = c - high - mid
    payload = jnp.concatenate(
        [
            (slots // 128).astype(F32),
            (slots % 128).astype(F32),
            high,
            mid,
            low,
            jnp.zeros((16 - 11, rows), F32),
        ],
        axis=0,
    ).astype(BF16)
    for k in range(n_dp):
        at = lax.broadcasted_iota(jnp.int32, (cap, rows), 0) + k * cap
        pick = jnp.where(at == place, 1.0, 0.0).astype(BF16)
        got = dot(payload, pick, NT)
        send[k] = jnp.concatenate(
            [
                got[0:1] * 128.0 + got[1:2],
                got[2:5] + got[5:8] + got[8:11],
                jnp.zeros((4, cap), F32),
            ],
            axis=0,
        )
    asks = []
    for k in range(1, n_dp):
        to = (d + k) % n_dp
        asks.append(
            remote(send.at[to], recv.at[d], rq_send.at[k], rq_recv.at[k], (to, p))
        )
        asks[-1].start()
    recv[d] = send[d]

    def widen(b, carry):
        load(b).wait()
        tab[pl.ds(pl.multiple_of(b * step, step), step), :] = stage[b % 2].astype(F32)

        @pl.when(b + 2 < blocks)
        def _():
            load(b + 2).start()

        return carry

    lax.fori_loop(0, blocks, widen, 0)

    for ask in asks:
        ask.wait()
    for i in range(n_dp):
        got = recv[i]
        idx_v[i : i + 1, :] = jnp.clip(got[0:1].astype(jnp.int32), 0, table.shape[0] - 1)
        req[i] = got
    to_smem = pltpu.make_async_copy(idx_v, idx_s, idx_sem)
    to_smem.start()
    to_smem.wait()

    onward, spread, late = [None] * 2, [None] * 2, [None] * 2

    def forward(layer):
        wa = wholes[layer]
        part = wa.at[p2, pl.ds(half * dx, half)]
        across[layer].wait_recv()
        onward[layer] = remote(
            part, part, ag_send.at[layer, 2], ag_recv.at[layer, 2], (d1, p)
        )
        spread[layer] = remote(
            part, part, ag_send.at[layer, 3], ag_recv.at[layer, 3], (d, p1)
        )
        onward[layer].start()
        spread[layer].start()

    span = xbuf.shape[0]
    total = n_dp * cap
    for j in range(total // span):

        def fill(o, carry):
            for u in range(8):
                r = o * 8 + u
                q = j * span + r
                s = idx_s[q // cap, q % cap]
                xbuf[pl.ds(r, 1), :] = tab[pl.ds(s, 1), :]
            return carry

        lax.fori_loop(0, span // 8, fill, 0)
        x_t[:, j * span : (j + 1) * span] = xbuf[...].T.astype(BF16)
        if j == total // span // 2:
            forward(0)
    forward(1)
    for layer in range(2):
        wa = wholes[layer]
        part = wa.at[p2, pl.ds(half * (1 - dx), half)]
        onward[layer].wait_recv()
        late[layer] = remote(
            part, part, ag_send.at[layer, 4], ag_recv.at[layer, 4], (d, p1)
        )
        late[layer].start()
    for layer in range(2):
        own[layer].wait()
        core[layer].wait()
        across[layer].wait_send()
        onward[layer].wait_send()
        spread[layer].wait()
        late[layer].wait()


def fetch(n_dp, cap, owner, slot, cot, ws1, ws2, table):
    rows, width = owner.shape[1], table.shape[1]
    total = n_dp * cap
    step = min(1024, table.shape[0])
    whole = (4,) + ws1.shape
    dma = pltpu.SemaphoreType.DMA
    vmem = pl.BlockSpec(memory_space=VMEM)
    hbm = pl.BlockSpec(memory_space=ANY)
    return pl.pallas_call(
        functools.partial(fetch_kernel, n_dp, cap),
        out_shape=[
            jax.ShapeDtypeStruct((width, total), BF16),
            jax.ShapeDtypeStruct((n_dp, 8, cap), F32),
            jax.ShapeDtypeStruct((1, rows), jnp.int32),
            jax.ShapeDtypeStruct(whole, BF16),
            jax.ShapeDtypeStruct(whole, BF16),
        ],
        in_specs=[vmem] * 3 + [hbm] * 3,
        out_specs=[vmem] * 3 + [hbm] * 2,
        scratch_shapes=[
            pltpu.VMEM((n_dp, 8, cap), F32),
            pltpu.VMEM((n_dp, 8, cap), F32),
            pltpu.VMEM((n_dp, cap), jnp.int32),
            pltpu.SMEM((n_dp, cap), jnp.int32),
            pltpu.VMEM((2, step, width), BF16),
            pltpu.VMEM((table.shape[0], width), F32),
            pltpu.VMEM((256, width), F32),
            dma((2,)),
            dma((2, 5)),
            dma((2, 5)),
            dma((n_dp,)),
            dma((n_dp,)),
            dma,
            dma((2,)),
        ],
        compiler_params=pltpu.CompilerParams(
            collective_id=0, has_side_effects=True, vmem_limit_bytes=50 * MIB
        ),
    )(owner, slot, cot, ws1, ws2, table)


def forward_kernel(tasks, x_t, wa, gate, bo, h, s, y, g, out, z):
    e = pl.program_id(0)
    wide = x_t.shape[1] // 128

    @pl.when(e == 0)
    def _():
        logits = dot(gate[...], x_t[...])
        for t in range(tasks):
            part = logits[8 * t : 8 * t + 8]
            top = jnp.exp(part - jnp.max(part, axis=0, keepdims=True))
            g[t] = top / jnp.sum(top, axis=0, keepdims=True)
        z[...] = jnp.zeros_like(z)

    block = wa[...].reshape(256, wa.shape[3])
    bias = block[:, 768:896].astype(F32)
    pre = dot(block[:, :512], x_t[...]) + jnp.concatenate([bias] * wide, axis=1)
    u = pre * 0.5
    th = jnp.tanh(u)
    a = 1.0 + th
    smooth = u * a
    hb = smooth.astype(BF16)
    h[0] = hb
    s[0] = (0.5 * (a + smooth * (1.0 - th))).astype(BF16)
    out_bias = bo[0].astype(F32)
    ye = dot(block[:, 512:768], hb, TN) + jnp.concatenate([out_bias] * wide, axis=1)
    y[0] = ye.astype(BF16)
    for t in range(tasks):
        z[t] += g[t, pl.ds(e, 1), :] * ye

    @pl.when(e == pl.num_programs(0) - 1)
    def _():
        for t in range(tasks):
            out[256 * t : 256 * t + 256, :] = z[t].astype(BF16)


def layer_forward(x_t, wa, gate, bo, tasks):
    total = x_t.shape[1]
    act = jax.ShapeDtypeStruct((8, 256, total), BF16)
    per = pl.BlockSpec((1, 256, total), lambda e: (e, 0, 0))
    return pl.pallas_call(
        functools.partial(forward_kernel, tasks),
        grid=(8,),
        out_shape=[
            act, act, act,
            jax.ShapeDtypeStruct((tasks, 8, total), F32),
            jax.ShapeDtypeStruct((256 * tasks, total), BF16),
        ],
        in_specs=[
            pl.BlockSpec(x_t.shape, lambda e: (0, 0)),
            pl.BlockSpec((4, 1, 64, wa.shape[3]), lambda e: (0, e, 0, 0)),
            pl.BlockSpec(gate.shape, lambda e: (0, 0)),
            pl.BlockSpec((1, 256, 128), lambda e: (e, 0, 0)),
        ],
        out_specs=[
            per, per, per,
            pl.BlockSpec((tasks, 8, total), lambda e: (0, 0, 0)),
            pl.BlockSpec((256 * tasks, total), lambda e: (0, 0)),
        ],
        scratch_shapes=[pltpu.VMEM((tasks, 256, total), F32)],
        compiler_params=pltpu.CompilerParams(vmem_limit_bytes=58 * MIB),
    )(x_t, wa, gate, bo)


def tower_kernel(zb, w, vec, cot, pred, dz, dw, sums):
    t = pl.program_id(0)
    wide = zb.shape[1] // 128

    def spread(v):
        return jnp.concatenate([v.astype(F32)] * wide, axis=1)

    zt, wt = zb[...], w[0]
    act = dot(wt, zt, TN) + spread(vec[0, 0])
    out_w = spread(vec[0, 1])
    sig = 0.5 + 0.5 * jnp.tanh(0.5 * act)
    smooth = act * sig
    logit = jnp.sum(smooth * out_w, axis=0, keepdims=True) + spread(vec[0, 2, 0:1])
    prob = jax.nn.sigmoid(logit)
    pred[pl.ds(t, 1), :] = prob
    dlogit = cot[pl.ds(t + 1, 1), :] * prob * (1.0 - prob)
    dact = dlogit * out_w * (sig + smooth * (1.0 - sig))
    dab = dact.astype(BF16)
    dz[...] = dot(wt, dab).astype(BF16)
    dw[...] = dot(dab, zt, NT)
    lane = lax.broadcasted_iota(jnp.int32, (128, 128), 1)
    one = jnp.sum(dact, axis=1, keepdims=True)
    two = jnp.sum(dlogit * smooth, axis=1, keepdims=True)
    three = jnp.sum(dlogit, axis=1, keepdims=True)
    sums[0] = jnp.where(lane == 0, one, jnp.where(lane == 1, two, three))


def towers(zb, w, vec, cot):
    total = zb.shape[1]
    return pl.pallas_call(
        tower_kernel,
        grid=(3,),
        out_shape=[
            jax.ShapeDtypeStruct((8, total), F32),
            jax.ShapeDtypeStruct((768, total), BF16),
            jax.ShapeDtypeStruct((128, 768), F32),
            jax.ShapeDtypeStruct((3, 128, 128), F32),
        ],
        in_specs=[
            pl.BlockSpec((256, total), lambda t: (t, 0)),
            pl.BlockSpec((1, 256, 128), lambda t: (t, 0, 0)),
            pl.BlockSpec((1, 3, 128, 128), lambda t: (t, 0, 0, 0)),
            pl.BlockSpec((8, total), lambda t: (0, 0)),
        ],
        out_specs=[
            pl.BlockSpec((8, total), lambda t: (0, 0)),
            pl.BlockSpec((256, total), lambda t: (t, 0)),
            pl.BlockSpec((128, 256), lambda t: (0, t)),
            pl.BlockSpec((1, 128, 128), lambda t: (t, 0, 0)),
        ],
        compiler_params=pltpu.CompilerParams(vmem_limit_bytes=58 * MIB),
    )(zb, w, vec, cot)


def backward_kernel(tasks, by_rows, x_t, wa, gate, g, dz, h, s, y, grads, dx, dgate, sums, acc, dg):
    e = pl.program_id(0)

    @pl.when(e == 0)
    def _():
        acc[...] = jnp.zeros_like(acc)
        sums[...] = jnp.zeros_like(sums)

    block = wa[...].reshape(256, wa.shape[3])
    ye = y[0].astype(F32)
    dy = None
    for t in range(tasks):
        dzt = dz[256 * t : 256 * t + 256, :].astype(F32)
        term = g[t, pl.ds(e, 1), :] * dzt
        dy = term if dy is None else dy + term
        dg[t, pl.ds(e, 1), :] = jnp.sum(dzt * ye, axis=0, keepdims=True)
    dyb = dy.astype(BF16)
    dpre = dot(block[:, 512:768], dyb) * s[0].astype(F32)
    dpb = dpre.astype(BF16)
    grads[0, :, 0:512] = dot(dpb, x_t[...], NT).astype(BF16)
    grads[0, :, 512:768] = dot(h[0], dyb, NT).astype(BF16)
    acc[...] += dot(block[:, :512], dpb, TN)
    lane = lax.broadcasted_iota(jnp.int32, (256, 128), 1)
    one = jnp.sum(dy, axis=1, keepdims=True)
    two = jnp.sum(dpre, axis=1, keepdims=True)
    sums[...] += jnp.where(lane == e, one, jnp.where(lane == e + 8, two, 0.0))

    @pl.when(e == pl.num_programs(0) - 1)
    def _():
        parts = []
        for t in range(tasks):
            gt, dgt = g[t], dg[t]
            parts.append(gt * (dgt - jnp.sum(gt * dgt, axis=0, keepdims=True)))
        dlogits = jnp.concatenate(parts, axis=0).astype(BF16)
        dgate[...] = dot(dlogits, x_t[...], NT)
        whole = acc[...] + dot(gate[...], dlogits, TN)
        if by_rows:
            for q in range(4):
                dx[q] = whole[128 * q : 128 * q + 128, :].T.astype(BF16)
        else:
            dx[...] = whole.astype(BF16)


def layer_backward(x_t, wa, gate, g, dz, h, s, y, tasks, by_rows):
    total = x_t.shape[1]
    per = pl.BlockSpec((1, 256, total), lambda e: (e, 0, 0))
    dx = (4, total, 128) if by_rows else (512, total)
    return pl.pallas_call(
        functools.partial(backward_kernel, tasks, by_rows),
        grid=(8,),
        out_shape=[
            jax.ShapeDtypeStruct((8, 256, 768), BF16),
            jax.ShapeDtypeStruct(dx, BF16),
            jax.ShapeDtypeStruct(gate.shape, F32),
            jax.ShapeDtypeStruct((256, 128), F32),
        ],
        in_specs=[
            pl.BlockSpec(x_t.shape, lambda e: (0, 0)),
            pl.BlockSpec((4, 1, 64, wa.shape[3]), lambda e: (0, e, 0, 0)),
            pl.BlockSpec(gate.shape, lambda e: (0, 0)),
            pl.BlockSpec(g.shape, lambda e: (0, 0, 0)),
            pl.BlockSpec(dz.shape, lambda e: (0, 0)),
            per, per, per,
        ],
        out_specs=[
            pl.BlockSpec((1, 256, 768), lambda e: (e, 0, 0)),
            pl.BlockSpec(dx, lambda e: (0,) * len(dx)),
            pl.BlockSpec(gate.shape, lambda e: (0, 0)),
            pl.BlockSpec((256, 128), lambda e: (0, 0)),
        ],
        scratch_shapes=[
            pltpu.VMEM((512, total), F32),
            pltpu.VMEM((tasks, 8, total), F32),
        ],
        compiler_params=pltpu.CompilerParams(vmem_limit_bytes=58 * MIB),
    )(x_t, wa, gate, g, dz, h, s, y)


UNITS = 9


def sum_kernel(
    n_dp, grads, dxq, req, pred, place,
    shard, shared, dx_all, req_all, pred_out,
    core_in, mine, y_in, half, x_in, quarter, z_in, piece, gathered, pred_send, pred_recv,
    sem_s, sem_r, z_send, z_recv, zz_send, zz_recv, dx_send, dx_recv, rq_send, rq_recv, p_send, p_recv, loc,
):
    d, p, p1, p2, d1 = partners(n_dp)
    deep = n_dp // 2
    full = deep == 4
    z, dx, py, pc = d // 2, d % 2, p // 2, p % 2
    cap = pred_send.shape[2]
    greet([((d + k) % n_dp, p) for k in range(1, n_dp)] + [(d, (p + k) % 4) for k in range(1, 4)])

    back = []
    for i in range(n_dp):
        pred_send[i] = pred[i]
    for k in range(1, n_dp):
        to = (d + k) % n_dp
        back.append(remote(pred_send.at[to], pred_recv.at[d], p_send.at[k], p_recv.at[k], (to, p)))
        back[-1].start()
    pred_recv[d] = pred_send[d]

    moves = []
    for k in range(1, 4):
        to = (p + k) % 4
        moves.append(remote(dxq.at[to], dx_all.at[p], dx_send.at[k], dx_recv.at[k], (d, to)))
        moves.append(remote(req, req_all.at[p], rq_send.at[k], rq_recv.at[k], (d, to)))
    keep = [
        pltpu.make_async_copy(dxq.at[p], dx_all.at[p], loc.at[0]),
        pltpu.make_async_copy(req, req_all.at[p], loc.at[1]),
    ]

    started = {}

    def go(name, copy):
        copy.start()
        started.setdefault(name, []).append(copy)

    def stage0(u):
        for yy in range(2):
            go((0, u), remote(
                grads.at[u, :, 2 * yy + (1 - pc)], core_in.at[u, yy],
                sem_s.at[u, yy], sem_r.at[u, yy], (d, p1)))

    def stage1(u):
        for copy in started[(0, u)]:
            copy.wait()
        for yy in range(2):
            mine[u, yy] = (
                grads[u, :, 2 * yy + pc].astype(F32) + core_in[u, yy].astype(F32)
            ).astype(BF16)
        go((1, u), remote(
            mine.at[u, 1 - py], y_in.at[u], sem_s.at[u, 2], sem_r.at[u, 2], (d, p2)))

    def stage2(u):
        for copy in started[(1, u)]:
            copy.wait()
        total = mine[u, py].astype(F32) + y_in[u].astype(F32)
        if not full:
            shard[u] = total
            return
        for xh in range(2):
            half[u, xh] = total[:, xh].astype(BF16)
        go((2, u), remote(
            half.at[u, 1 - dx], x_in.at[u], sem_s.at[u, 3], sem_r.at[u, 3], (d1, p)))

    def stage3(u):
        for copy in started[(2, u)]:
            copy.wait()
        quarter[u] = (half[u, dx].astype(F32) + x_in[u].astype(F32)).astype(BF16)
        for k in range(1, 4):
            to = (z + k) % 4
            go((3, u), remote(
                quarter.at[u, to // 2, to % 2], z_in.at[u, k],
                z_send.at[u, k], z_recv.at[u, k], (2 * to + dx, p)))

    def stage4(u):
        for copy in started[(3, u)]:
            copy.wait()
        total = quarter[u, z // 2, z % 2].astype(F32)
        for k in range(1, 4):
            total = total + z_in[u, k].astype(F32)
        piece[u] = total.astype(BF16)
        gathered[u, dx, z] = piece[u]
        for k in range(1, 4):
            to = (z + k) % 4
            go((4, u), remote(
                piece.at[u], gathered.at[u, dx, z],
                zz_send.at[u, k], zz_recv.at[u, k], (2 * to + dx, p)))

    def stage5(u):
        for copy in started[(4, u)]:
            copy.wait()
        go((5, u), remote(
            gathered.at[u, dx], gathered.at[u, dx], sem_s.at[u, 4], sem_r.at[u, 4], (d1, p)))

    def stage6(u):
        for copy in started[(5, u)]:
            copy.wait()
        for xh in range(2):
            for e in range(2):
                for zr in range(2):
                    shard[u, e, xh, zr] = gathered[u, xh, 2 * e + zr].astype(F32)

    stages = [stage0, stage1, stage2] + ([stage3, stage4, stage5, stage6] if full else [])
    for tick in range(UNITS + len(stages) - 1):
        for at in range(len(stages) - 1, -1, -1):
            u = tick - at
            if 0 <= u < UNITS:
                stages[at](u)
        if tick == 1:
            for move in moves + keep:
                move.start()
    last = UNITS - 1
    if full:
        shared[p] = gathered[last]
        again = [
            remote(gathered.at[last], shared.at[p], sem_s.at[k, 5], sem_r.at[k, 5], (d, (p + k) % 4))
            for k in range(1, 4)
        ]
        for copy in again:
            copy.start()
    else:
        again = []
    for copy in back:
        copy.wait()
    rows = place.shape[1]
    out = jnp.zeros((16, rows), F32)
    for i in range(n_dp):
        c = pred_recv[i]
        high = c.astype(BF16).astype(F32)
        low = c - high
        both = jnp.concatenate([high, low], axis=0).astype(BF16)
        at = lax.broadcasted_iota(jnp.int32, (cap, rows), 0) + i * cap
        pick = jnp.where(at == place[...], 1.0, 0.0).astype(BF16)
        out = out + dot(both, pick)
    pred_out[...] = (out[0:8] + out[8:16])[0:3]
    for copy in again:
        copy.wait()
    for move in moves + keep:
        move.wait()


def sum_up(n_dp, grads, dxq, req, pred, place):
    full = n_dp == 8
    cap = pred.shape[2]
    rows = place.shape[1]
    dma = pltpu.SemaphoreType.DMA
    vmem = pl.BlockSpec(memory_space=VMEM)
    hbm = pl.BlockSpec(memory_space=ANY)
    part = (2, 2, 16, 768)
    return pl.pallas_call(
        functools.partial(sum_kernel, n_dp),
        out_shape=[
            jax.ShapeDtypeStruct((UNITS, 2) + part, F32),
            jax.ShapeDtypeStruct((4, 2, 4, 16, 768), BF16),
            jax.ShapeDtypeStruct(dxq.shape, BF16),
            jax.ShapeDtypeStruct((4,) + req.shape, F32),
            jax.ShapeDtypeStruct((3, rows), F32),
        ],
        in_specs=[vmem, hbm, hbm, vmem, vmem],
        out_specs=[vmem, vmem, hbm, hbm, vmem],
        scratch_shapes=[
            pltpu.VMEM((UNITS, 2, 2) + part, BF16),
            pltpu.VMEM((UNITS, 2, 2) + part, BF16),
            pltpu.VMEM((UNITS, 2) + part, BF16),
            pltpu.VMEM((UNITS, 2, 2, 2, 16, 768), BF16),
            pltpu.VMEM((UNITS, 2, 2, 16, 768), BF16),
            pltpu.VMEM((UNITS, 2, 2, 16, 768), BF16),
            pltpu.VMEM((UNITS, 4, 16, 768), BF16),
            pltpu.VMEM((UNITS, 16, 768), BF16),
            pltpu.VMEM((UNITS, 2, 4, 16, 768), BF16),
            pltpu.VMEM((n_dp, 8, cap), F32),
            pltpu.VMEM((n_dp, 8, cap), F32),
            dma((UNITS, 6)),
            dma((UNITS, 6)),
            dma((UNITS, 4)),
            dma((UNITS, 4)),
            dma((UNITS, 4)),
            dma((UNITS, 4)),
            dma((4,)),
            dma((4,)),
            dma((4,)),
            dma((4,)),
            dma((n_dp,)),
            dma((n_dp,)),
            dma((2,)),
        ],
        compiler_params=pltpu.CompilerParams(
            collective_id=1, has_side_effects=True, vmem_limit_bytes=58 * MIB
        ),
    )(grads, dxq, req, pred, place)


def scatter_kernel(slots, dx, out, a0, a1, a2, a3, buf):
    parts = (a0, a1, a2, a3)
    span = buf.shape[1]
    for a in parts:
        a[...] = jnp.zeros_like(a)

    def block(j, carry):
        at = pl.multiple_of(j * span, span)
        for q in range(4):
            buf[q] = dx[q, pl.ds(at, span), :].astype(F32)

        def add(o, inner):
            for u in range(4):
                r = o * 4 + u
                for q in range(4):
                    to = pl.ds(slots[q, at + r], 1)
                    parts[q][to, :] += buf[q, pl.ds(r, 1), :]
            return inner

        lax.fori_loop(0, span // 4, add, 0)
        return carry

    lax.fori_loop(0, dx.shape[1] // span, block, 0)
    out[...] = (a0[...] + a1[...]) + (a2[...] + a3[...])


def scatter(slots, dx, rows):
    vmem = pl.BlockSpec(memory_space=VMEM)
    table = (rows, 128)
    return pl.pallas_call(
        scatter_kernel,
        out_shape=jax.ShapeDtypeStruct(table, F32),
        in_specs=[pl.BlockSpec(memory_space=pltpu.SMEM), vmem],
        out_specs=vmem,
        scratch_shapes=[pltpu.VMEM(table, F32)] * 4 + [pltpu.VMEM((4, 256, 128), F32)],
        compiler_params=pltpu.CompilerParams(vmem_limit_bytes=58 * MIB),
    )(slots, dx)


def shard_of(w_in, b_in, w_out):
    bias = jnp.broadcast_to(b_in[:, :, None], b_in.shape + (128,))
    return jnp.concatenate([w_in.transpose(1, 2, 0), w_out, bias], axis=2)


def on_device(
    owner, slot, table, w_in1, b_in1, w_out1, b_out1, gate1,
    w_in2, b_in2, w_out2, b_out2, gate2,
    tower_in, tower_bias, tower_out, tower_out_bias, pred_cot,
):
    n_dp = lax.axis_size("dp")
    rows = owner.shape[0]
    cap = 4 * rows // n_dp
    total = n_dp * cap
    x1, req, place, wa1, wa2 = fetch(
        n_dp,
        cap,
        owner.reshape(1, rows),
        slot.reshape(1, rows),
        pred_cot,
        shard_of(w_in1, b_in1, w_out1),
        shard_of(w_in2, b_in2, w_out2),
        table,
    )
    flat = req.transpose(1, 0, 2).reshape(8, total)
    bo1 = jnp.broadcast_to(b_out1[:, :, None], b_out1.shape + (128,))
    bo2 = jnp.broadcast_to(b_out2[:, :, None], b_out2.shape + (128,))
    g1t = gate1.reshape(gate1.shape[0], -1).T
    g2t = gate2.reshape(gate2.shape[0], -1).T
    vec = jnp.stack(
        [
            tower_bias,
            tower_out,
            jnp.broadcast_to(tower_out_bias[:, None], tower_out.shape),
        ],
        axis=1,
    )
    vec = jnp.broadcast_to(vec[:, :, :, None], vec.shape + (128,))
    h1, s1, y1, g1, x2 = layer_forward(x1, wa1, g1t, bo1, 2)
    h2, s2, y2, g2, zb = layer_forward(x2, wa2, g2t, bo2, 3)
    pred, dz2, dtower, tsums = towers(zb, tower_in, vec, flat)
    grads2, dz1, dgate2, sums2 = layer_backward(x2, wa2, g2t, g2, dz2, h2, s2, y2, 3, False)
    grads1, dxq, dgate1, sums1 = layer_backward(x1, wa1, g1t, g1, dz1, h1, s1, y1, 2, True)
    biases = jnp.concatenate([sums1[:, :16], sums2[:, :16]], axis=1).T
    gates = jnp.concatenate([dgate1, dgate2], axis=0)
    small = tsums[:, :, :3].transpose(2, 0, 1).reshape(3, 384)
    small = jnp.concatenate([small.reshape(1, -1), jnp.zeros((1, 768 * 2 - 1152), F32)], axis=1)
    small = small.reshape(2, 768)
    shared = jnp.concatenate(
        [
            dtower,
            jnp.concatenate([gates, jnp.pad(biases, ((0, 8), (0, 0)))], axis=1),
            small,
            jnp.zeros((512 - 128 - 40 - 2, 768), F32),
        ],
        axis=0,
    ).astype(BF16)
    grads = jnp.concatenate([grads2, grads1, shared.reshape(2, 256, 768)], axis=0)
    grads = grads.reshape(UNITS, 2, 4, 2, 2, 16, 768)
    by_source = pred.reshape(8, n_dp, cap).transpose(1, 0, 2)
    sums, whole, dx_all, req_all, predictions = sum_up(n_dp, grads, dxq, req, by_source, place)
    if n_dp == 8:
        whole = whole.reshape(4, 2, 2, 2, 16, 768).transpose(2, 0, 1, 3, 4, 5)
        whole = whole.reshape(512, 768).astype(F32)
    else:
        sums = lax.psum(sums, "dp")
        whole = lax.all_gather(sums[UNITS - 1], "mp", axis=0)
        whole = whole.transpose(1, 0, 2, 3, 4, 5).reshape(512, 768)
    sums = sums[: UNITS - 1].reshape(2, 8, 64, 768)
    slots = req_all[:, :, 0, :].reshape(4, total).astype(jnp.int32)
    table_grad = scatter(slots, dx_all, table.shape[0])
    dtower, gates, biases = whole[:128], whole[128:168, :512], whole[128:160, 512:]
    small = whole[168:170].reshape(-1)[:1152].reshape(3, 3, 128)
    inner = w_in1.shape[2]
    start = lax.axis_index("mp") * inner
    b_in = [lax.dynamic_slice_in_dim(biases[k : k + 8], start, inner, axis=1) for k in (8, 24)]
    w_in = [sums[k, :, :, :512].transpose(2, 0, 1) for k in (1, 0)]
    return (
        predictions,
        table_grad,
        w_in[0],
        b_in[0],
        sums[1, :, :, 512:],
        biases[0:8],
        gates[:16].T.reshape(gate1.shape),
        w_in[1],
        b_in[1],
        sums[0, :, :, 512:],
        biases[16:24],
        gates[16:40].T.reshape(gate2.shape),
        dtower.reshape(128, 3, 256).transpose(1, 2, 0),
        small[0],
        small[1],
        small[2, :, 0],
    )


def solution(mesh):
    in_specs = (
        P(("dp", "mp"), None),
        P(("dp", "mp")),
        P("dp", None),
        P(None, None, "mp"),
        P(None, "mp"),
        P(None, "mp", None),
        P(),
        P(),
        P(None, None, "mp"),
        P(None, "mp"),
        P(None, "mp", None),
        P(),
        P(),
        P(),
        P(),
        P(),
        P(),
        P(None, ("dp", "mp")),
    )
    out_specs = (
        P(None, ("dp", "mp")),
        P("dp", "mp"),
        P(None, None, "mp"),
        P(None, "mp"),
        P(None, "mp", None),
        P(),
        P(),
        P(None, None, "mp"),
        P(None, "mp"),
        P(None, "mp", None),
        P(),
        P(),
        P(),
        P(),
        P(),
        P(),
    )
    return jax.shard_map(
        on_device, mesh=mesh, in_specs=in_specs, out_specs=out_specs, check_vma=False
    )
```

```python
import functools

import jax
import jax.numpy as jnp
from jax import lax
from jax.experimental import pallas as pl
from jax.experimental.pallas import tpu as pltpu
from jax.sharding import PartitionSpec as P

F32, BF16 = jnp.float32, jnp.bfloat16
MESH = pl.DeviceIdType.MESH
MIB = 2**20
VMEM, ANY = pltpu.VMEM, pl.ANY
NN, NT, TN = ((1,), (0,)), ((1,), (1,)), ((0,), (0,))


def dot(a, b, dims=NN):
    return lax.dot_general(a, b, (dims, ((), ())), preferred_element_type=F32)


def remote(src, dst, send_sem, recv_sem, device):
    return pltpu.make_async_remote_copy(
        src_ref=src,
        dst_ref=dst,
        send_sem=send_sem,
        recv_sem=recv_sem,
        device_id=device,
        device_id_type=MESH,
    )


def greet(peers):
    barrier = pltpu.get_barrier_semaphore()
    for peer in peers:
        pl.semaphore_signal(barrier, inc=1, device_id=peer, device_id_type=MESH)
    pl.semaphore_wait(barrier, len(peers))


def partners(n_dp):
    d, p = lax.axis_index("dp"), lax.axis_index("mp")
    return d, p, p + 1 - 2 * (p % 2), (p + 2) % 4, d + 1 - 2 * (d % 2)


def fetch_kernel(
    n_dp, cap, owner, slot, cot, ws1, ws2, table,
    x_t, req, place_out, wa1, wa2,
    send, recv, idx_v, idx_s, stage, tab, xbuf,
    own_sem, ag_send, ag_recv, rq_send, rq_recv, idx_sem, tab_sem,
):
    d, p, p1, p2, d1 = partners(n_dp)
    rows = owner.shape[1]
    half = ws1.shape[0] // 2
    dx = d % 2
    blocks = table.shape[0] // stage.shape[1]
    step = stage.shape[1]

    def load(b):
        return pltpu.make_async_copy(
            table.at[pl.ds(b * step, step)], stage.at[b % 2], tab_sem.at[b % 2]
        )

    for b in range(min(2, blocks)):
        load(b).start()

    greet([((d + k) % n_dp, p) for k in range(1, n_dp)] + [(d, p1), (d, p2)])

    shards, wholes = (ws1, ws2), (wa1, wa2)
    own, core, across = [], [], []
    for layer in range(2):
        ws, wa = shards[layer], wholes[layer]
        own.append(pltpu.make_async_copy(ws, wa.at[p], own_sem.at[layer]))
        core.append(
            remote(ws, wa.at[p], ag_send.at[layer, 0], ag_recv.at[layer, 0], (d, p1))
        )
        mine = pl.ds(half * dx, half)
        across.append(
            remote(
                ws.at[mine], wa.at[p, mine], ag_send.at[layer, 1], ag_recv.at[layer, 1], (d, p2)
            )
        )
        across[layer].start()
        own[layer].start()
        core[layer].start()

    own_row = owner[...]
    count = max(8, n_dp)
    ks = lax.broadcasted_iota(jnp.int32, (count, rows), 0)
    onehot = jnp.where(ks == own_row, 1.0, 0.0)
    upper = jnp.where(
        lax.broadcasted_iota(jnp.int32, (rows, rows), 0)
        < lax.broadcasted_iota(jnp.int32, (rows, rows), 1),
        1.0,
        0.0,
    ).astype(BF16)
    before = dot(onehot.astype(BF16), upper)
    rank = jnp.sum(before * onehot, axis=0, keepdims=True).astype(jnp.int32)
    place = own_row * cap + rank
    place_out[...] = place
    slots = slot[...]
    c = cot[...]
    high = c.astype(BF16).astype(F32)
    mid = (c - high).astype(BF16).astype(F32)
    low = c - high - mid
    payload = jnp.concatenate(
        [
            (slots // 128).astype(F32),
            (slots % 128).astype(F32),
            high,
            mid,
            low,
            jnp.zeros((16 - 11, rows), F32),
        ],
        axis=0,
    ).astype(BF16)
    for k in range(n_dp):
        at = lax.broadcasted_iota(jnp.int32, (cap, rows), 0) + k * cap
        pick = jnp.where(at == place, 1.0, 0.0).astype(BF16)
        got = dot(payload, pick, NT)
        send[k] = jnp.concatenate(
            [
                got[0:1] * 128.0 + got[1:2],
                got[2:5] + got[5:8] + got[8:11],
                jnp.zeros((4, cap), F32),
            ],
            axis=0,
        )
    asks = []
    for k in range(1, n_dp):
        to = (d + k) % n_dp
        asks.append(
            remote(send.at[to], recv.at[d], rq_send.at[k], rq_recv.at[k], (to, p))
        )
        asks[-1].start()
    recv[d] = send[d]

    def widen(b, carry):
        load(b).wait()
        tab[pl.ds(pl.multiple_of(b * step, step), step), :] = stage[b % 2].astype(F32)

        @pl.when(b + 2 < blocks)
        def _():
            load(b + 2).start()

        return carry

    lax.fori_loop(0, blocks, widen, 0)

    for ask in asks:
        ask.wait()
    for i in range(n_dp):
        got = recv[i]
        idx_v[i : i + 1, :] = jnp.clip(got[0:1].astype(jnp.int32), 0, table.shape[0] - 1)
        req[i] = got
    to_smem = pltpu.make_async_copy(idx_v, idx_s, idx_sem)
    to_smem.start()
    to_smem.wait()

    onward, spread, late = [None] * 2, [None] * 2, [None] * 2

    def forward(layer):
        wa = wholes[layer]
        part = wa.at[p2, pl.ds(half * dx, half)]
        across[layer].wait_recv()
        onward[layer] = remote(
            part, part, ag_send.at[layer, 2], ag_recv.at[layer, 2], (d1, p)
        )
        spread[layer] = remote(
            part, part, ag_send.at[layer, 3], ag_recv.at[layer, 3], (d, p1)
        )
        onward[layer].start()
        spread[layer].start()

    span = xbuf.shape[0]
    total = n_dp * cap
    for j in range(total // span):

        def fill(o, carry):
            for u in range(8):
                r = o * 8 + u
                q = j * span + r
                s = idx_s[q // cap, q % cap]
                xbuf[pl.ds(r, 1), :] = tab[pl.ds(s, 1), :]
            return carry

        lax.fori_loop(0, span // 8, fill, 0)
        x_t[:, j * span : (j + 1) * span] = xbuf[...].T.astype(BF16)
        if j == total // span // 2:
            forward(0)
    forward(1)
    for layer in range(2):
        wa = wholes[layer]
        part = wa.at[p2, pl.ds(half * (1 - dx), half)]
        onward[layer].wait_recv()
        late[layer] = remote(
            part, part, ag_send.at[layer, 4], ag_recv.at[layer, 4], (d, p1)
        )
        late[layer].start()
    for layer in range(2):
        own[layer].wait()
        core[layer].wait()
        across[layer].wait_send()
        onward[layer].wait_send()
        spread[layer].wait()
        late[layer].wait()


def fetch(n_dp, cap, owner, slot, cot, ws1, ws2, table):
    rows, width = owner.shape[1], table.shape[1]
    total = n_dp * cap
    step = min(1024, table.shape[0])
    whole = (4,) + ws1.shape
    dma = pltpu.SemaphoreType.DMA
    vmem = pl.BlockSpec(memory_space=VMEM)
    hbm = pl.BlockSpec(memory_space=ANY)
    return pl.pallas_call(
        functools.partial(fetch_kernel, n_dp, cap),
        out_shape=[
            jax.ShapeDtypeStruct((width, total), BF16),
            jax.ShapeDtypeStruct((n_dp, 8, cap), F32),
            jax.ShapeDtypeStruct((1, rows), jnp.int32),
            jax.ShapeDtypeStruct(whole, BF16),
            jax.ShapeDtypeStruct(whole, BF16),
        ],
        in_specs=[vmem] * 3 + [hbm] * 3,
        out_specs=[vmem] * 3 + [hbm] * 2,
        scratch_shapes=[
            pltpu.VMEM((n_dp, 8, cap), F32),
            pltpu.VMEM((n_dp, 8, cap), F32),
            pltpu.VMEM((n_dp, cap), jnp.int32),
            pltpu.SMEM((n_dp, cap), jnp.int32),
            pltpu.VMEM((2, step, width), BF16),
            pltpu.VMEM((table.shape[0], width), F32),
            pltpu.VMEM((256, width), F32),
            dma((2,)),
            dma((2, 5)),
            dma((2, 5)),
            dma((n_dp,)),
            dma((n_dp,)),
            dma,
            dma((2,)),
        ],
        compiler_params=pltpu.CompilerParams(
            collective_id=0, has_side_effects=True, vmem_limit_bytes=50 * MIB
        ),
    )(owner, slot, cot, ws1, ws2, table)


def forward_kernel(tasks, x_t, wa, gate, bo, h, s, y, g, out, z):
    e = pl.program_id(0)
    wide = x_t.shape[1] // 128

    @pl.when(e == 0)
    def _():
        logits = dot(gate[...], x_t[...])
        for t in range(tasks):
            part = logits[8 * t : 8 * t + 8]
            top = jnp.exp(part - jnp.max(part, axis=0, keepdims=True))
            g[t] = top / jnp.sum(top, axis=0, keepdims=True)
        z[...] = jnp.zeros_like(z)

    block = wa[...].reshape(256, wa.shape[3])
    bias = block[:, 768:896].astype(F32)
    pre = dot(block[:, :512], x_t[...]) + jnp.concatenate([bias] * wide, axis=1)
    u = pre * 0.5
    th = jnp.tanh(u)
    a = 1.0 + th
    smooth = u * a
    hb = smooth.astype(BF16)
    h[0] = hb
    s[0] = (0.5 * (a + smooth * (1.0 - th))).astype(BF16)
    out_bias = bo[0].astype(F32)
    ye = dot(block[:, 512:768], hb, TN) + jnp.concatenate([out_bias] * wide, axis=1)
    y[0] = ye.astype(BF16)
    for t in range(tasks):
        z[t] += g[t, pl.ds(e, 1), :] * ye

    @pl.when(e == pl.num_programs(0) - 1)
    def _():
        for t in range(tasks):
            out[256 * t : 256 * t + 256, :] = z[t].astype(BF16)


def layer_forward(x_t, wa, gate, bo, tasks):
    total = x_t.shape[1]
    act = jax.ShapeDtypeStruct((8, 256, total), BF16)
    per = pl.BlockSpec((1, 256, total), lambda e: (e, 0, 0))
    return pl.pallas_call(
        functools.partial(forward_kernel, tasks),
        grid=(8,),
        out_shape=[
            act, act, act,
            jax.ShapeDtypeStruct((tasks, 8, total), F32),
            jax.ShapeDtypeStruct((256 * tasks, total), BF16),
        ],
        in_specs=[
            pl.BlockSpec(x_t.shape, lambda e: (0, 0)),
            pl.BlockSpec((4, 1, 64, wa.shape[3]), lambda e: (0, e, 0, 0)),
            pl.BlockSpec(gate.shape, lambda e: (0, 0)),
            pl.BlockSpec((1, 256, 128), lambda e: (e, 0, 0)),
        ],
        out_specs=[
            per, per, per,
            pl.BlockSpec((tasks, 8, total), lambda e: (0, 0, 0)),
            pl.BlockSpec((256 * tasks, total), lambda e: (0, 0)),
        ],
        scratch_shapes=[pltpu.VMEM((tasks, 256, total), F32)],
        compiler_params=pltpu.CompilerParams(vmem_limit_bytes=58 * MIB),
    )(x_t, wa, gate, bo)


def tower_kernel(zb, w, vec, cot, pred, dz, dw, sums):
    t = pl.program_id(0)
    wide = zb.shape[1] // 128

    def spread(v):
        return jnp.concatenate([v.astype(F32)] * wide, axis=1)

    zt, wt = zb[...], w[0]
    act = dot(wt, zt, TN) + spread(vec[0, 0])
    out_w = spread(vec[0, 1])
    sig = 0.5 + 0.5 * jnp.tanh(0.5 * act)
    smooth = act * sig
    logit = jnp.sum(smooth * out_w, axis=0, keepdims=True) + spread(vec[0, 2, 0:1])
    prob = jax.nn.sigmoid(logit)
    pred[pl.ds(t, 1), :] = prob
    dlogit = cot[pl.ds(t + 1, 1), :] * prob * (1.0 - prob)
    dact = dlogit * out_w * (sig + smooth * (1.0 - sig))
    dab = dact.astype(BF16)
    dz[...] = dot(wt, dab).astype(BF16)
    dw[...] = dot(dab, zt, NT)
    lane = lax.broadcasted_iota(jnp.int32, (128, 128), 1)
    one = jnp.sum(dact, axis=1, keepdims=True)
    two = jnp.sum(dlogit * smooth, axis=1, keepdims=True)
    three = jnp.sum(dlogit, axis=1, keepdims=True)
    table = jnp.where(lane == 0, one, jnp.where(lane == 1, two, three))
    sums[0] = table.T[0:8]


def towers(zb, w, vec, cot):
    total = zb.shape[1]
    return pl.pallas_call(
        tower_kernel,
        grid=(3,),
        out_shape=[
            jax.ShapeDtypeStruct((8, total), F32),
            jax.ShapeDtypeStruct((768, total), BF16),
            jax.ShapeDtypeStruct((128, 768), F32),
            jax.ShapeDtypeStruct((3, 8, 128), F32),
        ],
        in_specs=[
            pl.BlockSpec((256, total), lambda t: (t, 0)),
            pl.BlockSpec((1, 256, 128), lambda t: (t, 0, 0)),
            pl.BlockSpec((1, 3, 128, 128), lambda t: (t, 0, 0, 0)),
            pl.BlockSpec((8, total), lambda t: (0, 0)),
        ],
        out_specs=[
            pl.BlockSpec((8, total), lambda t: (0, 0)),
            pl.BlockSpec((256, total), lambda t: (t, 0)),
            pl.BlockSpec((128, 256), lambda t: (0, t)),
            pl.BlockSpec((1, 8, 128), lambda t: (t, 0, 0)),
        ],
        compiler_params=pltpu.CompilerParams(vmem_limit_bytes=58 * MIB),
    )(zb, w, vec, cot)


def back_kernel(
    n_dp, x1, x2, wa1, wa2, gate1, gate2, g1, g2, dz2, h1, s1, y1, h2, s2, y2,
    dtower, tsums, req, pred, place,
    summed, shared, dx_all, req_all, pred_out,
    acc, dz1, dg, sums, dgate, dxq, *rest,
):
    main, small, links = rest[:10], rest[10:20], rest[20:]
    pred_send, pred_recv = links[:2]
    sem_s, sem_r, z_s, z_r, zz_s, zz_r, dx_s, dx_r, rq_s, rq_r, p_s, p_r, again_s, again_r, loc = links[2:]
    step = pl.program_id(0)
    d, p, p1, p2, d1 = partners(n_dp)
    full = n_dp == 8
    z, dx, py, pc = d // 2, d % 2, p // 2, p % 2
    cap = pred_send.shape[2]
    grads = main[0]
    units = grads.shape[0]

    def copies(stage, u):
        bufs, i = (main, u) if u < units else (small, 0)
        own, core_in, mine, y_in, half, x_in, quarter, z_in, piece, gathered = bufs
        if stage == 0:
            return [
                remote(
                    own.at[i, :, 2 * yy + (1 - pc)], core_in.at[i, yy],
                    sem_s.at[u, yy], sem_r.at[u, yy], (d, p1),
                )
                for yy in range(2)
            ]
        if stage == 1:
            return [remote(mine.at[i, 1 - py], y_in.at[i], sem_s.at[u, 2], sem_r.at[u, 2], (d, p2))]
        if stage == 2:
            return [remote(half.at[i, 1 - dx], x_in.at[i], sem_s.at[u, 3], sem_r.at[u, 3], (d1, p))]
        if stage == 3:
            return [
                remote(
                    quarter.at[i, (z + k) % 4 // 2, (z + k) % 4 % 2], z_in.at[i, k],
                    z_s.at[u, k], z_r.at[u, k], (2 * ((z + k) % 4) + dx, p),
                )
                for k in range(1, 4)
            ]
        if stage == 4:
            return [
                remote(
                    piece.at[i], gathered.at[i, dx, z],
                    zz_s.at[u, k], zz_r.at[u, k], (2 * ((z + k) % 4) + dx, p),
                )
                for k in range(1, 4)
            ]
        part = gathered.at[i, dx]
        return [remote(part, part, sem_s.at[u, 4], sem_r.at[u, 4], (d1, p))]

    def advance(stage, u):
        bufs, i = (main, u) if u < units else (small, 0)
        own, core_in, mine, y_in, half, x_in, quarter, z_in, piece, gathered = bufs
        if stage:
            for copy in copies(stage - 1, u):
                copy.wait()
        if stage == 1:
            for yy in range(2):
                both = own[i, :, 2 * yy + pc].astype(F32) + core_in[i, yy].astype(F32)
                mine[i, yy] = both.astype(BF16)
        if stage == 2:
            both = mine[i, py].astype(F32) + y_in[i].astype(F32)
            for xh in range(2):
                half[i, xh] = both[:, xh].astype(BF16)
        if stage == 3:
            quarter[i] = (half[i, dx].astype(F32) + x_in[i].astype(F32)).astype(BF16)
        if stage == 4:
            both = quarter[i, z // 2, z % 2].astype(F32)
            for k in range(1, 4):
                both = both + z_in[i, k].astype(F32)
            piece[i] = both.astype(BF16)
            gathered[i, dx, z] = piece[i]
        if stage < last_stage:
            for copy in copies(stage, u):
                copy.start()

    last_stage = 6 if full else 2

    def tick(at, count):
        for stage in range(last_stage, -1, -1):
            u = at - stage
            if 0 <= u < count:
                advance(stage, u)

    def predictions_back():
        return [
            remote(
                pred_send.at[(d + k) % n_dp], pred_recv.at[d], p_s.at[k], p_r.at[k],
                ((d + k) % n_dp, p),
            )
            for k in range(1, n_dp)
        ]

    def requests_over():
        return [
            remote(req, req_all.at[p], rq_s.at[k], rq_r.at[k], (d, (p + k) % 4))
            for k in range(1, 4)
        ] + [pltpu.make_async_copy(req, req_all.at[p], loc.at[1])]

    def columns_over():
        return [
            remote(dxq.at[(p + k) % 4], dx_all.at[p], dx_s.at[k], dx_r.at[k], (d, (p + k) % 4))
            for k in range(1, 4)
        ] + [pltpu.make_async_copy(dxq.at[p], dx_all.at[p], loc.at[0])]

    @pl.when(step == 0)
    def _():
        greet(
            [((d + k) % n_dp, p) for k in range(1, n_dp)]
            + [(d, (p + k) % 4) for k in range(1, 4)]
        )
        for i in range(n_dp):
            pred_send[i] = pred[i]
        for copy in predictions_back() + requests_over():
            copy.start()
        pred_recv[d] = pred_send[d]
        sums[...] = jnp.zeros_like(sums)

    def expert(tasks, e, lanes, x_t, wa, g, dz, h, s, y):
        block = wa[...].reshape(256, wa.shape[3])
        ye = y[0].astype(F32)
        dy = None
        for t in range(tasks):
            dzt = dz[256 * t : 256 * t + 256, :].astype(F32)
            term = g[t, pl.ds(e, 1), :] * dzt
            dy = term if dy is None else dy + term
            dg[t, pl.ds(e, 1), :] = jnp.sum(dzt * ye, axis=0, keepdims=True)
        dyb = dy.astype(BF16)
        dpre = dot(block[:, 512:768], dyb) * s[0].astype(F32)
        dpb = dpre.astype(BF16)
        split = (4, 2, 2, 16)
        grads[step // 2, step % 2, :, :, :, :, 0:512] = (
            dot(dpb, x_t[...], NT).astype(BF16).reshape(split + (512,))
        )
        grads[step // 2, step % 2, :, :, :, :, 512:768] = (
            dot(h[0], dyb, NT).astype(BF16).reshape(split + (256,))
        )
        prod = dot(block[:, :512], dpb, TN)

        @pl.when(e == 0)
        def _():
            acc[...] = prod

        @pl.when(e > 0)
        def _():
            acc[...] += prod

        lane = lax.broadcasted_iota(jnp.int32, (256, 128), 1)
        one = jnp.sum(dy, axis=1, keepdims=True)
        two = jnp.sum(dpre, axis=1, keepdims=True)
        sums[...] += jnp.where(
            lane == lanes + e, one, jnp.where(lane == lanes + 8 + e, two, 0.0)
        )

    def finish(tasks, first, x_t, gate, g):
        parts = []
        for t in range(tasks):
            gt, dgt = g[t], dg[t]
            parts.append(gt * (dgt - jnp.sum(gt * dgt, axis=0, keepdims=True)))
        dlogits = jnp.concatenate(parts, axis=0).astype(BF16)
        dgate[first : first + 8 * tasks] = dot(dlogits, x_t[...], NT)
        return acc[...] + dot(gate[...], dlogits, TN)

    @pl.when(step < 8)
    def _():
        expert(3, step, 16, x2, wa2, g2, dz2, h2, s2, y2)

    @pl.when(step == 7)
    def _():
        dz1[...] = finish(3, 16, x2, gate2, g2).astype(BF16)

    @pl.when(step >= 8)
    def _():
        expert(2, step - 8, 0, x1, wa1, g1, dz1, h1, s1, y1)

    for at in range(units):

        @pl.when(step == 2 * at + 1)
        def _(at=at):
            tick(at, units)

    @pl.when(step == 2 * units - 1)
    def _():
        whole = finish(2, 0, x1, gate1, g1)
        for q in range(4):
            dxq[q] = whole[128 * q : 128 * q + 128, :].T.astype(BF16)
        own = small[0]
        block = (2, 2, 2, 16, 256)
        for t in range(3):
            tower = dtower[:, 256 * t : 256 * t + 256].astype(BF16).reshape(block)
            own[0, t // 2, 2 * (t % 2) : 2 * (t % 2) + 2] = tower
        gates = dgate[...]
        tail = jnp.concatenate(
            [
                gates[:, :256],
                gates[:, 256:],
                sums[...].T[:32],
                jnp.concatenate([tsums[0], tsums[1]], axis=1),
                jnp.concatenate([tsums[2], jnp.zeros((8, 128), F32)], axis=1),
            ],
            axis=0,
        )
        own[0, 1, 2:4] = tail.astype(BF16).reshape(block)
        for at in range(units, units + last_stage + 1):
            tick(at, units + 1)
            if at == units + 1:
                for copy in columns_over():
                    copy.start()
        gathered = small[9]

        def again():
            return [
                remote(gathered.at[0], shared.at[p], again_s.at[k], again_r.at[k], (d, (p + k) % 4))
                for k in range(1, 4)
            ] + [pltpu.make_async_copy(gathered.at[0], shared.at[p], loc.at[2])]

        result = main[9] if full else main[2]
        out = pltpu.make_async_copy(result, summed, loc.at[3])
        if full:
            for copy in again():
                copy.start()
        else:
            for u in range(units):
                result[u, 0] = main[4][u].reshape(result.shape[2:])
            pltpu.make_async_copy(small[4].at[0], shared.at[0], loc.at[2]).start()
        out.start()
        for copy in predictions_back():
            copy.wait()
        rows = place.shape[1]
        got = jnp.zeros((16, rows), F32)
        for i in range(n_dp):
            c = pred_recv[i]
            high = c.astype(BF16).astype(F32)
            both = jnp.concatenate([high, c - high], axis=0).astype(BF16)
            at = lax.broadcasted_iota(jnp.int32, (cap, rows), 0) + i * cap
            pick = jnp.where(at == place[...], 1.0, 0.0).astype(BF16)
            got = got + dot(both, pick)
        pred_out[...] = (got[0:8] + got[8:16])[0:3]
        for copy in requests_over() + columns_over():
            copy.wait()
        if full:
            for copy in again():
                copy.wait()
        else:
            pltpu.make_async_copy(small[4].at[0], shared.at[0], loc.at[2]).wait()
        out.wait()


def backward(n_dp, x1, x2, wa1, wa2, gate1, gate2, g1, g2, dz2, l1, l2, dtower, tsums, req, pred, place):
    total = x1.shape[1]
    cap, rows = pred.shape[2], place.shape[1]
    full = n_dp == 8
    dma = pltpu.SemaphoreType.DMA
    hbm = pl.BlockSpec(memory_space=ANY)

    def fixed(a):
        return pl.BlockSpec(a.shape, lambda i: (0,) * a.ndim, pipeline_mode=pl.Buffered(1))

    first, second = (lambda i: jnp.maximum(i - 8, 0)), (lambda i: jnp.minimum(i, 7))
    per1 = pl.BlockSpec((1, 256, total), lambda i: (first(i), 0, 0))
    per2 = pl.BlockSpec((1, 256, total), lambda i: (second(i), 0, 0))

    def buffers(units, lanes):
        part = (2, 2, 2, 16, lanes)
        shapes = [
            (units, 2, 4) + part[1:],
            (units, 2) + part,
            (units, 2) + part,
            (units,) + part,
            (units, 2, 2, 2, 16, lanes),
            (units, 2, 2, 16, lanes),
            (units, 2, 2, 16, lanes),
            (units, 4, 16, lanes),
            (units, 16, lanes),
            (units, 2, 4, 16, lanes),
        ]
        return [pltpu.VMEM(shape, BF16) for shape in shapes]

    units = 8
    return pl.pallas_call(
        functools.partial(back_kernel, n_dp),
        grid=(2 * units,),
        out_shape=[
            jax.ShapeDtypeStruct((units, 2, 4, 16, 768) if full else (units, 2, 2, 2, 2, 16, 768), BF16),
            jax.ShapeDtypeStruct((4, 2, 4, 16, 256) if full else (1, 2, 2, 2, 16, 256), BF16),
            jax.ShapeDtypeStruct((4, total, 128), BF16),
            jax.ShapeDtypeStruct((4,) + req.shape, F32),
            jax.ShapeDtypeStruct((3, rows), F32),
        ],
        in_specs=[
            fixed(x1),
            fixed(x2),
            pl.BlockSpec((4, 1, 64, wa1.shape[3]), lambda i: (0, first(i), 0, 0)),
            pl.BlockSpec((4, 1, 64, wa2.shape[3]), lambda i: (0, second(i), 0, 0)),
            fixed(gate1), fixed(gate2), fixed(g1), fixed(g2), fixed(dz2),
            per1, per1, per1, per2, per2, per2,
            fixed(dtower), fixed(tsums), hbm, fixed(pred), fixed(place),
        ],
        out_specs=[hbm, hbm, hbm, hbm, pl.BlockSpec((3, rows), lambda i: (0, 0))],
        scratch_shapes=[
            pltpu.VMEM((512, total), F32),
            pltpu.VMEM((512, total), BF16),
            pltpu.VMEM((3, 8, total), F32),
            pltpu.VMEM((256, 128), F32),
            pltpu.VMEM((40, 512), F32),
            pltpu.VMEM((4, total, 128), BF16),
        ]
        + buffers(units, 768)
        + buffers(1, 256)
        + [
            pltpu.VMEM((n_dp, 8, cap), F32),
            pltpu.VMEM((n_dp, 8, cap), F32),
            dma((units + 1, 5)),
            dma((units + 1, 5)),
            dma((units + 1, 4)),
            dma((units + 1, 4)),
            dma((units + 1, 4)),
            dma((units + 1, 4)),
            dma((4,)),
            dma((4,)),
            dma((4,)),
            dma((4,)),
            dma((n_dp,)),
            dma((n_dp,)),
            dma((4,)),
            dma((4,)),
            dma((4,)),
        ],
        compiler_params=pltpu.CompilerParams(
            collective_id=1, has_side_effects=True, vmem_limit_bytes=62 * MIB
        ),
    )(
        x1, x2, wa1, wa2, gate1, gate2, g1, g2, dz2, *l1, *l2, dtower, tsums, req, pred, place
    )


def scatter_kernel(slots, dx, out, a0, a1, a2, a3, buf):
    parts = (a0, a1, a2, a3)
    span = buf.shape[1]
    for a in parts:
        a[...] = jnp.zeros_like(a)

    def block(j, carry):
        at = pl.multiple_of(j * span, span)
        for q in range(4):
            buf[q] = dx[q, pl.ds(at, span), :].astype(F32)

        def add(o, inner):
            for u in range(4):
                r = o * 4 + u
                for q in range(4):
                    to = pl.ds(slots[q, at + r], 1)
                    parts[q][to, :] += buf[q, pl.ds(r, 1), :]
            return inner

        lax.fori_loop(0, span // 4, add, 0)
        return carry

    lax.fori_loop(0, dx.shape[1] // span, block, 0)
    out[...] = (a0[...] + a1[...]) + (a2[...] + a3[...])


def scatter(slots, dx, rows):
    vmem = pl.BlockSpec(memory_space=VMEM)
    table = (rows, 128)
    return pl.pallas_call(
        scatter_kernel,
        out_shape=jax.ShapeDtypeStruct(table, F32),
        in_specs=[pl.BlockSpec(memory_space=pltpu.SMEM), vmem],
        out_specs=vmem,
        scratch_shapes=[pltpu.VMEM(table, F32)] * 4 + [pltpu.VMEM((4, 256, 128), F32)],
        compiler_params=pltpu.CompilerParams(vmem_limit_bytes=58 * MIB),
    )(slots, dx)


def shard_of(w_in, b_in, w_out):
    bias = jnp.broadcast_to(b_in[:, :, None], b_in.shape + (128,))
    return jnp.concatenate([w_in.transpose(1, 2, 0), w_out, bias], axis=2)


def on_device(
    owner, slot, table, w_in1, b_in1, w_out1, b_out1, gate1,
    w_in2, b_in2, w_out2, b_out2, gate2,
    tower_in, tower_bias, tower_out, tower_out_bias, pred_cot,
):
    n_dp = lax.axis_size("dp")
    rows = owner.shape[0]
    cap = 4 * rows // n_dp
    total = n_dp * cap
    x1, req, place, wa1, wa2 = fetch(
        n_dp,
        cap,
        owner.reshape(1, rows),
        slot.reshape(1, rows),
        pred_cot,
        shard_of(w_in1, b_in1, w_out1),
        shard_of(w_in2, b_in2, w_out2),
        table,
    )
    flat = req.transpose(1, 0, 2).reshape(8, total)
    bo1 = jnp.broadcast_to(b_out1[:, :, None], b_out1.shape + (128,))
    bo2 = jnp.broadcast_to(b_out2[:, :, None], b_out2.shape + (128,))
    g1t = gate1.reshape(gate1.shape[0], -1).T
    g2t = gate2.reshape(gate2.shape[0], -1).T
    vec = jnp.stack(
        [
            tower_bias,
            tower_out,
            jnp.broadcast_to(tower_out_bias[:, None], tower_out.shape),
        ],
        axis=1,
    )
    vec = jnp.broadcast_to(vec[:, :, :, None], vec.shape + (128,))
    h1, s1, y1, g1, x2 = layer_forward(x1, wa1, g1t, bo1, 2)
    h2, s2, y2, g2, zb = layer_forward(x2, wa2, g2t, bo2, 3)
    pred, dz2, dtower, tsums = towers(zb, tower_in, vec, flat)
    by_source = pred.reshape(8, n_dp, cap).transpose(1, 0, 2)
    sums, whole, dx_all, req_all, predictions = backward(
        n_dp, x1, x2, wa1, wa2, g1t, g2t, g1, g2, dz2, (h1, s1, y1), (h2, s2, y2),
        dtower, tsums, req, by_source, place,
    )
    if n_dp == 8:
        sums = sums.reshape(2, 4, 2, 2, 2, 16, 768).transpose(0, 1, 3, 2, 4, 5, 6).astype(F32)
        whole = whole.reshape(4, 2, 2, 2, 16, 256).transpose(2, 0, 1, 3, 4, 5)
    else:
        sums = lax.psum(sums[:, 0].astype(F32), "dp")
        sums = sums.reshape(2, 4, 2, 2, 2, 16, 768).transpose(0, 1, 3, 2, 4, 5, 6)
        whole = lax.all_gather(lax.psum(whole[0].astype(F32), "dp"), "mp", axis=0)
        whole = whole.transpose(2, 0, 1, 3, 4, 5)
    whole = whole.reshape(512, 256).astype(F32)
    sums = sums.reshape(2, 8, 64, 768)
    slots = req_all[:, :, 0, :].reshape(4, total).astype(jnp.int32)
    table_grad = scatter(slots, dx_all, table.shape[0])
    dtower = whole[:384].reshape(3, 128, 256).transpose(0, 2, 1)
    gates = jnp.concatenate([whole[384:424], whole[424:464]], axis=1)
    biases = whole[464:496]
    small = jnp.stack([whole[496:499, :128], whole[496:499, 128:], whole[504:507, :128]], axis=1)
    inner = w_in1.shape[2]
    start = lax.axis_index("mp") * inner
    b_in = [lax.dynamic_slice_in_dim(biases[k : k + 8], start, inner, axis=1) for k in (8, 24)]
    w_in = [sums[k, :, :, :512].transpose(2, 0, 1) for k in (1, 0)]
    return (
        predictions,
        table_grad,
        w_in[0],
        b_in[0],
        sums[1, :, :, 512:],
        biases[0:8],
        gates[:16].T.reshape(gate1.shape),
        w_in[1],
        b_in[1],
        sums[0, :, :, 512:],
        biases[16:24],
        gates[16:40].T.reshape(gate2.shape),
        dtower,
        small[0],
        small[1],
        small[2, :, 0],
    )


def solution(mesh):
    in_specs = (
        P(("dp", "mp"), None),
        P(("dp", "mp")),
        P("dp", None),
        P(None, None, "mp"),
        P(None, "mp"),
        P(None, "mp", None),
        P(),
        P(),
        P(None, None, "mp"),
        P(None, "mp"),
        P(None, "mp", None),
        P(),
        P(),
        P(),
        P(),
        P(),
        P(),
        P(None, ("dp", "mp")),
    )
    out_specs = (
        P(None, ("dp", "mp")),
        P("dp", "mp"),
        P(None, None, "mp"),
        P(None, "mp"),
        P(None, "mp", None),
        P(),
        P(),
        P(None, None, "mp"),
        P(None, "mp"),
        P(None, "mp", None),
        P(),
        P(),
        P(),
        P(),
        P(),
        P(),
    )
    return jax.shard_map(
        on_device, mesh=mesh, in_specs=in_specs, out_specs=out_specs, check_vma=False
    )
```

```python
import functools

import jax
import jax.numpy as jnp
from jax import lax
from jax.experimental import pallas as pl
from jax.experimental.pallas import tpu as pltpu
from jax.sharding import PartitionSpec as P

F32, BF16 = jnp.float32, jnp.bfloat16
MESH = pl.DeviceIdType.MESH
MIB = 2**20
VMEM, ANY = pltpu.VMEM, pl.ANY
NN, NT, TN = ((1,), (0,)), ((1,), (1,)), ((0,), (0,))
LAGS = {True: (0, 1, 4, 6, 8, 10, 12), False: (0, 1, 4, 6, 8, 10, 12)}


def dot(a, b, dims=NN):
    return lax.dot_general(a, b, (dims, ((), ())), preferred_element_type=F32)


def remote(src, dst, send_sem, recv_sem, device):
    return pltpu.make_async_remote_copy(
        src_ref=src,
        dst_ref=dst,
        send_sem=send_sem,
        recv_sem=recv_sem,
        device_id=device,
        device_id_type=MESH,
    )


def greet(peers):
    barrier = pltpu.get_barrier_semaphore()
    for peer in peers:
        pl.semaphore_signal(barrier, inc=1, device_id=peer, device_id_type=MESH)
    pl.semaphore_wait(barrier, len(peers))


def partners(n_dp):
    d, p = lax.axis_index("dp"), lax.axis_index("mp")
    return d, p, p + 1 - 2 * (p % 2), (p + 2) % 4, d + 1 - 2 * (d % 2)


def column(cols, at):
    lane = lax.broadcasted_iota(jnp.int32, cols.shape, 1)
    return jnp.sum(jnp.where(lane == at, cols, 0.0), axis=1, keepdims=True)


def front_kernel(
    n_dp, cap,
    owner, slot, cot, b_in1, b_in2, b_out1, b_out2, tower_bias, tower_out, tower_last, gate1, gate2, tower_w,
    ws1, ws2, table,
    x1_out, x2_out, wa_out, hsy_out, dz2_out, slots, place_out, g1, g2, pred, dtower, tsums,
    x1, x2, wa, hsy, dz2, cols, bias, send, recv, idx_s, stage, tab, xbuf, z, cot_rows,
    own_sem, core_s, core_r, y_s, y_r, x_s, x_r, near_s, near_r, late_s, late_r,
    bias_s, bias_r, rq_s, rq_r, idx_sem, tab_sem, out_sem, hsy_sem, dz_sem,
):
    d, p, p1, p2, d1 = partners(n_dp)
    rows = owner.shape[1]
    experts = ws1.shape[0]
    half = experts // 2
    dx = d % 2
    shards = (ws1, ws2)
    total = n_dp * cap

    def own_part(layer):
        return pltpu.make_async_copy(shards[layer], wa.at[layer, p], own_sem.at[layer])

    def core_part(layer):
        return remote(
            shards[layer], wa.at[layer, p], core_s.at[layer], core_r.at[layer], (d, p1)
        )

    def span_of(side, chunk):
        return pl.ds(half * side + half // 2 * chunk, half // 2)

    def y_part(layer, c):
        at = span_of(dx, c)
        return remote(
            shards[layer].at[at], wa.at[layer, p, at], y_s.at[layer, c], y_r.at[layer, c], (d, p2)
        )

    def onward(side, c, layer, sems, device):
        part = wa.at[layer, p2, span_of(side, c)]
        return remote(part, part, sems[0].at[layer, c], sems[1].at[layer, c], device)

    def x_part(layer, c):
        return onward(dx, c, layer, (x_s, x_r), (d1, p))

    def near_part(layer, c):
        return onward(dx, c, layer, (near_s, near_r), (d, p1))

    def late_part(layer, c):
        return onward(1 - dx, c, layer, (late_s, late_r), (d, p1))

    def bias_parts():
        return [
            remote(bias.at[p], bias.at[p], bias_s.at[k], bias_r.at[k], (d, (p + k) % 4))
            for k in range(1, 4)
        ]

    def forward_on(layer, c):
        y_part(layer, c).wait_recv()
        x_part(layer, c).start()
        near_part(layer, c).start()

    def finish_on(layer, c):
        x_part(layer, c).wait_recv()
        late_part(layer, c).start()

    def arrived(layer):
        own_part(layer).wait()
        core_part(layer).wait_recv()
        for c in range(2):
            near_part(layer, c).wait_recv()
            late_part(layer, c).wait_recv()

    def sent(layer):
        core_part(layer).wait_send()
        for c in range(2):
            for part in (y_part, x_part, near_part, late_part):
                part(layer, c).wait_send()

    def gather_all():
        step = stage.shape[1]
        blocks = table.shape[0] // step

        def load(b):
            return pltpu.make_async_copy(
                table.at[pl.ds(b * step, step)], stage.at[b % 2], tab_sem.at[b % 2]
            )

        for b in range(min(2, blocks)):
            load(b).start()
        greet(
            [((d + k) % n_dp, p) for k in range(1, n_dp)]
            + [(d, (p + k) % 4) for k in range(1, 4)]
        )
        for c in range(2):
            y_part(0, c).start()
        core_part(0).start()
        own_part(0).start()
        def as_columns(parts, wide):
            both = jnp.concatenate([part[...].astype(F32) for part in parts], axis=0)
            high = both.shape[0]
            both = jnp.concatenate([both, jnp.zeros((128 - high, both.shape[1]), F32)], axis=0)
            if both.shape[1] < wide:
                both = jnp.concatenate([both, jnp.zeros((128, wide - both.shape[1]), F32)], axis=1)
            return both.T

        bias[p] = as_columns([b_in1, b_in2], 128)[0:64]
        for copy in bias_parts():
            copy.start()
        cols[0:256] = as_columns([b_out1, b_out2], 256)
        lane = lax.broadcasted_iota(jnp.int32, (3, 128), 0)
        last = tower_last[...].astype(F32)
        spread = jnp.zeros((3, 128), F32)
        for t in range(3):
            spread = jnp.where(lane == t, last[:, t : t + 1], spread)
        vectors = [tower_bias[...].astype(F32), tower_out[...].astype(F32), spread]
        cols[256:384] = as_columns(vectors, 128)

        own_row = owner[...]
        count = max(8, n_dp)
        ks = lax.broadcasted_iota(jnp.int32, (count, rows), 0)
        onehot = jnp.where(ks == own_row, 1.0, 0.0)
        upper = jnp.where(
            lax.broadcasted_iota(jnp.int32, (rows, rows), 0)
            < lax.broadcasted_iota(jnp.int32, (rows, rows), 1),
            1.0,
            0.0,
        ).astype(BF16)
        before = dot(onehot.astype(BF16), upper)
        rank = jnp.sum(before * onehot, axis=0, keepdims=True).astype(jnp.int32)
        place = own_row * cap + rank
        place_out[...] = place
        wanted = slot[...]
        c = cot[...]
        high = c.astype(BF16).astype(F32)
        mid = (c - high).astype(BF16).astype(F32)
        payload = jnp.concatenate(
            [
                (wanted // 128).astype(F32),
                (wanted % 128).astype(F32),
                high,
                mid,
                c - high - mid,
                jnp.zeros((16 - 11, rows), F32),
            ],
            axis=0,
        ).astype(BF16)
        for k in range(n_dp):
            at = lax.broadcasted_iota(jnp.int32, (cap, rows), 0) + k * cap
            pick = jnp.where(at == place, 1.0, 0.0).astype(BF16)
            got = dot(payload, pick, NT)
            send[k] = jnp.concatenate(
                [
                    got[0:1] * 128.0 + got[1:2],
                    got[2:5] + got[5:8] + got[8:11],
                    jnp.zeros((4, cap), F32),
                ],
                axis=0,
            )
        asks = [
            remote(
                send.at[(d + k) % n_dp], recv.at[d], rq_s.at[k], rq_r.at[k], ((d + k) % n_dp, p)
            )
            for k in range(1, n_dp)
        ]
        for ask in asks:
            ask.start()
        recv[d] = send[d]
        core_part(1).start()
        own_part(1).start()

        def widen(b, carry):
            load(b).wait()
            tab[pl.ds(pl.multiple_of(b * step, step), step), :] = stage[b % 2].astype(F32)

            @pl.when(b + 2 < blocks)
            def _():
                load(b + 2).start()

            return carry

        forward_on(0, 0)
        lax.fori_loop(0, blocks, widen, 0)
        forward_on(0, 1)
        for c in range(2):
            y_part(1, c).start()
        for ask in asks:
            ask.wait()
        for i in range(n_dp):
            got = recv[i]
            slots[i : i + 1, :] = jnp.clip(got[0:1].astype(jnp.int32), 0, table.shape[0] - 1)
            cot_rows[:, i * cap : (i + 1) * cap] = got
        to_smem = pltpu.make_async_copy(slots, idx_s, idx_sem)
        to_smem.start()
        to_smem.wait()

        span = xbuf.shape[0]
        for j in range(total // span):

            for i in range(span // cap):

                def fill(o, carry, i=i, j=j):
                    into = xbuf.at[pl.ds(pl.multiple_of(i * cap + o * 16, 16), 16)]
                    for u in range(16):
                        at = idx_s[j * (span // cap) + i, o * 16 + u]
                        into[u : u + 1, :] = tab[pl.ds(at, 1), :]
                    return carry

                lax.fori_loop(0, cap // 16, fill, 0)
            x1[:, j * span : (j + 1) * span] = xbuf[...].T.astype(BF16)
        for c in range(2):
            finish_on(0, c)
        arrived(0)
        for copy in bias_parts():
            copy.wait()

    def begin(tasks, x_t, gate, g):
        z[...] = jnp.zeros_like(z)
        logits = dot(gate[...], x_t[...])
        for t in range(tasks):
            part = logits[8 * t : 8 * t + 8]
            top = jnp.exp(part - jnp.max(part, axis=0, keepdims=True))
            g[t] = top / jnp.sum(top, axis=0, keepdims=True)

    def hsy_part(n):
        return pltpu.make_async_copy(hsy.at[n % 2], hsy_out.at[n], hsy_sem.at[n % 2])

    def expert(layer, tasks, e, x_t, g):
        n = experts * layer + e
        at = n % 2
        block = wa[layer, :, e].reshape(256, wa.shape[-1])
        both = bias[...].reshape(256, 128)
        pre = dot(block[:, :512], x_t[...]) + column(both, 8 * layer + e)
        u = pre * 0.5
        th = jnp.tanh(u)
        a = 1.0 + th
        smooth = u * a
        hb = smooth.astype(BF16)
        hsy[at, 0] = hb
        hsy[at, 1] = (0.5 * (a + smooth * (1.0 - th))).astype(BF16)
        ye = dot(block[:, 512:768], hb, TN) + column(cols[0:256], 8 * layer + e)
        hsy[at, 2] = ye.astype(BF16)

        for t in range(tasks):
            z[t] += g[t, pl.ds(e, 1), :] * ye
        hsy_part(n).start()

    def out_part(k):
        src = (x1, x2, wa.at[0], wa.at[1])[k]
        dst = (x1_out, x2_out, wa_out.at[0], wa_out.at[1])[k]
        return pltpu.make_async_copy(src, dst, out_sem.at[k])

    def dz_part(t):
        at = pl.ds(256 * t, 256)
        return pltpu.make_async_copy(dz2.at[at], dz2_out.at[at], dz_sem.at[t])

    gather_all()
    begin(2, x1, gate1, g1)
    out_part(0).start()
    out_part(2).start()

    def first_layer(e, carry):
        @pl.when(e >= 2)
        def _():
            hsy_part(e - 2).wait()

        expert(0, 2, e, x1, g1)
        for c in range(2):

            @pl.when(e == c)
            def _(c=c):
                forward_on(1, c)

            @pl.when(e == 4 + c)
            def _(c=c):
                finish_on(1, c)

        return carry

    lax.fori_loop(0, experts, first_layer, 0)
    for t in range(2):
        x2[256 * t : 256 * t + 256, :] = z[t].astype(BF16)
    out_part(1).start()
    arrived(1)
    out_part(3).start()
    begin(3, x2, gate2, g2)

    def second_layer(e, carry):
        hsy_part(experts + e - 2).wait()
        expert(1, 3, e, x2, g2)
        return carry

    lax.fori_loop(0, experts, second_layer, 0)
    for t in range(3):
        vec = cols[256:384]
        zt, wt = z[t].astype(BF16), tower_w[t]
        act = dot(wt, zt, TN) + column(vec, t)
        out_w = column(vec, t + 3)
        sig = 0.5 + 0.5 * jnp.tanh(0.5 * act)
        smooth = act * sig
        logit = jnp.sum(smooth * out_w, axis=0, keepdims=True) + column(vec, t + 6)[0:1]
        prob = jax.nn.sigmoid(logit)
        for i in range(n_dp):
            pred[i, t : t + 1, :] = prob[:, i * cap : (i + 1) * cap]
        dlogit = cot_rows[t + 1 : t + 2, :] * prob * (1.0 - prob)
        dact = dlogit * out_w * (sig + smooth * (1.0 - sig))
        dab = dact.astype(BF16)
        dz2[256 * t : 256 * t + 256, :] = dot(wt, dab).astype(BF16)
        dz_part(t).start()
        dtower[:, 256 * t : 256 * t + 256] = dot(dab, zt, NT)
        lane = lax.broadcasted_iota(jnp.int32, (128, 128), 1)
        one = jnp.sum(dact, axis=1, keepdims=True)
        two = jnp.sum(dlogit * smooth, axis=1, keepdims=True)
        three = jnp.sum(dlogit, axis=1, keepdims=True)
        both = jnp.where(lane == 0, one, jnp.where(lane == 1, two, three))
        tsums[t] = both.T[0:8]
    for layer in range(2):
        sent(layer)
    for n in (2 * experts - 2, 2 * experts - 1):
        hsy_part(n).wait()
    for k in range(4):
        out_part(k).wait()
    for t in range(3):
        dz_part(t).wait()


def front(n_dp, cap, small, ws1, ws2, table):
    rows, width = small[0].shape[1], table.shape[1]
    total = n_dp * cap
    step = min(1024, table.shape[0])
    whole = (4,) + ws1.shape
    dma = pltpu.SemaphoreType.DMA
    hbm = pl.BlockSpec(memory_space=ANY)
    vmem = pl.BlockSpec(memory_space=VMEM)
    shapes = [
        ((width, total), BF16),
        ((512, total), BF16),
        ((2,) + whole, BF16),
        ((16, 3, 256, total), BF16),
        ((768, total), BF16),
        ((n_dp, cap), jnp.int32),
        ((1, rows), jnp.int32),
        ((2, 8, total), F32),
        ((3, 8, total), F32),
        ((n_dp, 8, cap), F32),
        ((128, 768), F32),
        ((3, 8, 128), F32),
    ]
    return pl.pallas_call(
        functools.partial(front_kernel, n_dp, cap),
        out_shape=[jax.ShapeDtypeStruct(*s) for s in shapes],
        in_specs=[vmem] * len(small) + [hbm] * 3,
        out_specs=[hbm] * 5 + [vmem] * 7,
        scratch_shapes=[
            pltpu.VMEM((width, total), BF16),
            pltpu.VMEM((512, total), BF16),
            pltpu.VMEM((2,) + whole, BF16),
            pltpu.VMEM((2, 3, 256, total), BF16),
            pltpu.VMEM((768, total), BF16),
            pltpu.VMEM((384, 128), F32),
            pltpu.VMEM((4, 64, 128), F32),
            pltpu.VMEM((n_dp, 8, cap), F32),
            pltpu.VMEM((n_dp, 8, cap), F32),
            pltpu.SMEM((n_dp, cap), jnp.int32),
            pltpu.VMEM((2, step, width), BF16),
            pltpu.VMEM((table.shape[0], width), F32),
            pltpu.VMEM((max(256, cap), width), F32),
            pltpu.VMEM((3, 256, total), F32),
            pltpu.VMEM((8, total), F32),
            dma((2,)),
            dma((2,)),
            dma((2,)),
        ]
        + [dma((2, 2))] * 8
        + [dma((4,)), dma((4,)), dma((n_dp,)), dma((n_dp,)), dma, dma((2,))]
        + [dma((4,)), dma((2,)), dma((3,))],
        compiler_params=pltpu.CompilerParams(
            collective_id=0, has_side_effects=True, vmem_limit_bytes=62 * MIB
        ),
    )(*small, ws1, ws2, table)


def back_kernel(
    n_dp, gate1, gate2, g1, g2, dtower, tsums, pred, place, x1_in, x2_in, wa_in, dz2_in, hsy_in, slots,
    pred_out, summed, shared, dx_all, slots_all,
    x1, x2, wa, dz2, hsy, dpre_all, dz1, dg, sums, dgate, dxq, *rest,
):
    main, small, links = rest[:10], rest[10:20], rest[20:]
    pred_send, pred_recv = links[:2]
    (
        sem_s, sem_r, z_s, z_r, zz_s, zz_r, dx_s, dx_r, rq_s, rq_r, p_s, p_r, again_s, again_r, loc,
        in_sem, hsy_sem,
    ) = links[2:]
    d, p, p1, p2, d1 = partners(n_dp)
    full = n_dp == 8
    z, dx, py, pc = d // 2, d % 2, p // 2, p % 2
    cap = pred_send.shape[2]
    grads = main[0]
    units = grads.shape[0]

    def bufs_of(u):
        return (main, u) if u < units else (small, 0)

    def y_first(u):
        return u < units // 2 or not full

    def copies(stage, u):
        bufs, i = bufs_of(u)
        own, core_in, mine, one_in, half, two_in, quarter, z_in, piece, gathered = bufs
        over_y, over_x = (d, p2), (d1, p)
        if stage == 0:
            return [
                remote(
                    own.at[i, :, 2 * yy + (1 - pc)], core_in.at[i, yy],
                    sem_s.at[u, yy], sem_r.at[u, yy], (d, p1),
                )
                for yy in range(2)
            ]
        if stage == 1:
            if y_first(u):
                src, device = mine.at[i, 1 - py], over_y
            else:
                src, device = mine.at[i, :, :, 1 - dx], over_x
            return [remote(src, one_in.at[i], sem_s.at[u, 2], sem_r.at[u, 2], device)]
        if stage == 2:
            src, device = (1 - dx, over_x) if y_first(u) else (1 - py, over_y)
            return [remote(half.at[i, src], two_in.at[i], sem_s.at[u, 3], sem_r.at[u, 3], device)]
        if stage == 3:
            return [
                remote(
                    quarter.at[i, (z + k) % 4 // 2, (z + k) % 4 % 2], z_in.at[i, k],
                    z_s.at[u, k], z_r.at[u, k], (2 * ((z + k) % 4) + dx, p),
                )
                for k in range(1, 4)
            ]
        if stage == 4:
            return [
                remote(
                    piece.at[i], gathered.at[i, dx, z],
                    zz_s.at[u, k], zz_r.at[u, k], (2 * ((z + k) % 4) + dx, p),
                )
                for k in range(1, 4)
            ]
        part = gathered.at[i, dx]
        return [remote(part, part, sem_s.at[u, 4], sem_r.at[u, 4], (d1, p))]

    def advance(stage, u):
        bufs, i = bufs_of(u)
        own, core_in, mine, one_in, half, two_in, quarter, z_in, piece, gathered = bufs
        if stage:
            for copy in copies(stage - 1, u):
                copy.wait()
        if stage == 1:
            for yy in range(2):
                both = own[i, :, 2 * yy + pc].astype(F32) + core_in[i, yy].astype(F32)
                mine[i, yy] = both.astype(BF16)
        if stage == 2 and y_first(u):
            both = mine[i, py].astype(F32) + one_in[i].astype(F32)
            for xh in range(2):
                half[i, xh] = both[:, xh].astype(BF16)
        elif stage == 2:
            both = mine[i, :, :, dx].astype(F32) + one_in[i].astype(F32)
            half[i] = both.astype(BF16)
        if stage == 3:
            kept = half[i, dx if y_first(u) else py]
            quarter[i] = (kept.astype(F32) + two_in[i].astype(F32)).astype(BF16)
        if stage == 4:
            both = quarter[i, z // 2, z % 2].astype(F32)
            for k in range(1, 4):
                both = both + z_in[i, k].astype(F32)
            piece[i] = both.astype(BF16)
            gathered[i, dx, z] = piece[i]
        if stage < last_stage:
            for copy in copies(stage, u):
                copy.start()

    last_stage = 6 if full else 2

    last_step = 2 * units - 1

    def at_step(u, stage):
        whole_at = min(2 * u + 1, last_step)
        return whole_at + LAGS[y_first(u)][stage]

    def tick(at):
        for stage in range(last_stage, -1, -1):
            for u in range(units):
                if at_step(u, stage) == at:
                    advance(stage, u)

    def rounds():
        left = [
            [stage for stage in range(last_stage + 1) if at_step(u, stage) > last_step]
            for u in range(units + 1)
        ]
        for turn in range(max(cuts, last_stage + 1)):
            for u in range(units + 1):
                if turn < len(left[u]):
                    advance(left[u][turn], u)
            yield turn

    def predictions_back():
        return [
            remote(
                pred_send.at[(d + k) % n_dp], pred_recv.at[d], p_s.at[k], p_r.at[k],
                ((d + k) % n_dp, p),
            )
            for k in range(1, n_dp)
        ]

    def slots_over():
        return [
            remote(slots, slots_all.at[p], rq_s.at[k], rq_r.at[k], (d, (p + k) % 4))
            for k in range(1, 4)
        ] + [pltpu.make_async_copy(slots, slots_all.at[p], loc.at[1])]

    cut = 512
    cuts = x1.shape[1] // cut

    def columns_over(c):
        rows = pl.ds(c * cut, cut)
        return [
            remote(
                dxq.at[(p + k) % 4, rows], dx_all.at[p, rows],
                dx_s.at[c, k], dx_r.at[c, k], (d, (p + k) % 4),
            )
            for k in range(1, 4)
        ] + [pltpu.make_async_copy(dxq.at[p, rows], dx_all.at[p, rows], dx_s.at[c, 0])]

    def load(k):
        src = (dz2_in, x2_in, wa_in.at[1], x1_in, wa_in.at[0])[k]
        dst = (dz2, x2, wa.at[1], x1, wa.at[0])[k]
        return pltpu.make_async_copy(src, dst, in_sem.at[k])

    def hsy_load(n):
        return pltpu.make_async_copy(hsy_in.at[(n + 8) % 16], hsy.at[n % 2], hsy_sem.at[n % 2])

    hsy_load(0).start()
    for k in range(5):
        load(k).start()
    sums[...] = jnp.zeros_like(sums)
    greet(
        [((d + k) % n_dp, p) for k in range(1, n_dp)]
        + [(d, (p + k) % 4) for k in range(1, 4)]
    )
    for i in range(n_dp):
        pred_send[i] = pred[i]
    for copy in predictions_back() + slots_over():
        copy.start()
    pred_recv[d] = pred_send[d]

    def expert(layer, tasks, e, lanes, step, x_t, g, dz):
        at = step % 2
        w_out = wa[layer, :, e, :, 512:768].reshape(256, 256)
        ye = hsy[at, 2].astype(F32)
        dy = None
        for t in range(tasks):
            dzt = dz[256 * t : 256 * t + 256, :].astype(F32)
            term = g[t, pl.ds(e, 1), :] * dzt
            dy = term if dy is None else dy + term
            dg[t, pl.ds(e, 1), :] = jnp.sum(dzt * ye, axis=0, keepdims=True)
        dyb = dy.astype(BF16)
        dpre = dot(w_out, dyb) * hsy[at, 1].astype(F32)
        dpb = dpre.astype(BF16)
        dpre_all[e] = dpb
        split = (4, 2, 2, 16)
        grads[step // 2, step % 2, :, :, :, :, 0:512] = (
            dot(dpb, x_t[...], NT).astype(BF16).reshape(split + (512,))
        )
        grads[step // 2, step % 2, :, :, :, :, 512:768] = (
            dot(hsy[at, 0], dyb, NT).astype(BF16).reshape(split + (256,))
        )
        lane = lax.broadcasted_iota(jnp.int32, (256, 128), 1)
        one = jnp.sum(dy, axis=1, keepdims=True)
        two = jnp.sum(dpre, axis=1, keepdims=True)
        sums[...] += jnp.where(
            lane == lanes + e, one, jnp.where(lane == lanes + 8 + e, two, 0.0)
        )

    def gate_part(tasks, g):
        parts = []
        for t in range(tasks):
            gt, dgt = g[t], dg[t]
            parts.append(gt * (dgt - jnp.sum(gt * dgt, axis=0, keepdims=True)))
        return jnp.concatenate(parts, axis=0).astype(BF16)

    def input_grad(layer, c, gate, dlogits):
        at = slice(c * cut, (c + 1) * cut)
        w_in = wa[layer, :, :, :, 0:512].swapaxes(0, 1).reshape(2048, 512)
        part = dot(w_in, dpre_all[:, :, at].reshape(2048, cut), TN)
        return part + dot(gate[...], dlogits[:, at], TN)

    def one_step(layer, tasks, e, lanes, step, x_t, g, dz):
        hsy_load(step).wait()

        @pl.when(step < last_step)
        def _():
            hsy_load(step + 1).start()

        expert(layer, tasks, e, lanes, step, x_t, g, dz)

    def second_layer(e, carry):
        one_step(1, 3, e, 16, e, x2, g2, dz2)
        for at in range(8):

            @pl.when(e == at)
            def _(at=at):
                tick(at)

        return carry

    def first_layer(e, carry):
        one_step(0, 2, e, 0, 8 + e, x1, g1, dz1)
        for at in range(8):

            @pl.when(e == at)
            def _(at=at):
                tick(8 + at)

        return carry

    for k in range(3):
        load(k).wait()
    lax.fori_loop(0, 8, second_layer, 0)
    dlogits = gate_part(3, g2)
    dgate[16:40] = dot(dlogits, x2[...], NT)
    for c in range(cuts):
        dz1[:, c * cut : (c + 1) * cut] = input_grad(1, c, gate2, dlogits).astype(BF16)
    for k in range(3, 5):
        load(k).wait()
    lax.fori_loop(0, 8, first_layer, 0)
    dlogits = gate_part(2, g1)
    dgate[0:16] = dot(dlogits, x1[...], NT)
    own = small[0]
    block = (2, 2, 2, 16, 256)
    for t in range(3):
        tower = dtower[:, 256 * t : 256 * t + 256].astype(BF16).reshape(block)
        own[0, t // 2, 2 * (t % 2) : 2 * (t % 2) + 2] = tower
    gates = dgate[...]
    tail = jnp.concatenate(
        [
            gates[:, :256],
            gates[:, 256:],
            sums[...].T[:32],
            jnp.concatenate([tsums[0], tsums[1]], axis=1),
            jnp.concatenate([tsums[2], jnp.zeros((8, 128), F32)], axis=1),
        ],
        axis=0,
    )
    own[0, 1, 2:4] = tail.astype(BF16).reshape(block)
    advance(0, units)
    for turn in rounds():
        if turn < cuts:
            whole = input_grad(0, turn, gate1, dlogits)
            for q in range(4):
                block = whole[128 * q : 128 * q + 128, :]
                dxq[q, turn * cut : (turn + 1) * cut] = block.T.astype(BF16)
            for copy in columns_over(turn):
                copy.start()
    gathered = small[9]

    def again():
        return [
            remote(gathered.at[0], shared.at[p], again_s.at[k], again_r.at[k], (d, (p + k) % 4))
            for k in range(1, 4)
        ] + [pltpu.make_async_copy(gathered.at[0], shared.at[p], loc.at[2])]

    result = main[9] if full else main[2]
    out = pltpu.make_async_copy(result, summed, loc.at[3])
    if full:
        for copy in again():
            copy.start()
    else:
        for u in range(units):
            result[u, 0] = main[4][u].reshape(result.shape[2:])
        pltpu.make_async_copy(small[4].at[0], shared.at[0], loc.at[2]).start()
    out.start()
    for copy in predictions_back():
        copy.wait()
    rows = place.shape[1]
    got = jnp.zeros((16, rows), F32)
    for i in range(n_dp):
        c = pred_recv[i]
        high = c.astype(BF16).astype(F32)
        both = jnp.concatenate([high, c - high], axis=0).astype(BF16)
        at = lax.broadcasted_iota(jnp.int32, (cap, rows), 0) + i * cap
        pick = jnp.where(at == place[...], 1.0, 0.0).astype(BF16)
        got = got + dot(both, pick)
    pred_out[...] = (got[0:8] + got[8:16])[0:3]
    for copy in slots_over():
        copy.wait()
    for c in range(cuts):
        for copy in columns_over(c):
            copy.wait()
    if full:
        for copy in again():
            copy.wait()
    else:
        pltpu.make_async_copy(small[4].at[0], shared.at[0], loc.at[2]).wait()
    out.wait()


def backward(
    n_dp, gate1, gate2, g1, g2, dtower, tsums, pred, place, x1, x2, wa, dz2, hsy, slots
):
    total = x1.shape[1]
    cap, rows = pred.shape[2], place.shape[1]
    full = n_dp == 8
    dma = pltpu.SemaphoreType.DMA
    hbm = pl.BlockSpec(memory_space=ANY)
    vmem = pl.BlockSpec(memory_space=VMEM)

    def buffers(units, lanes):
        part = (2, 2, 2, 16, lanes)
        shapes = [
            (units, 2, 4) + part[1:],
            (units, 2) + part,
            (units, 2) + part,
            (units,) + part,
            (units, 2, 2, 2, 16, lanes),
            (units, 2, 2, 16, lanes),
            (units, 2, 2, 16, lanes),
            (units, 4, 16, lanes),
            (units, 16, lanes),
            (units, 2, 4, 16, lanes),
        ]
        return [pltpu.VMEM(shape, BF16) for shape in shapes]

    units = 8
    return pl.pallas_call(
        functools.partial(back_kernel, n_dp),
        out_shape=[
            jax.ShapeDtypeStruct((3, rows), F32),
            jax.ShapeDtypeStruct((units, 2, 4, 16, 768) if full else (units, 2, 2, 2, 2, 16, 768), BF16),
            jax.ShapeDtypeStruct((4, 2, 4, 16, 256) if full else (1, 2, 2, 2, 16, 256), BF16),
            jax.ShapeDtypeStruct((4, total, 128), BF16),
            jax.ShapeDtypeStruct((4,) + slots.shape, jnp.int32),
        ],
        in_specs=[vmem] * 8 + [hbm] * 6,
        out_specs=[vmem] + [hbm] * 4,
        scratch_shapes=[
            pltpu.VMEM(x1.shape, BF16),
            pltpu.VMEM(x2.shape, BF16),
            pltpu.VMEM(wa.shape, BF16),
            pltpu.VMEM(dz2.shape, BF16),
            pltpu.VMEM((2,) + hsy.shape[1:], BF16),
            pltpu.VMEM((8, 256, total), BF16),
            pltpu.VMEM((512, total), BF16),
            pltpu.VMEM((3, 8, total), F32),
            pltpu.VMEM((256, 128), F32),
            pltpu.VMEM((40, 512), F32),
            pltpu.VMEM((4, total, 128), BF16),
        ]
        + buffers(units, 768)
        + buffers(1, 256)
        + [
            pltpu.VMEM((n_dp, 8, cap), F32),
            pltpu.VMEM((n_dp, 8, cap), F32),
            dma((units + 1, 5)),
            dma((units + 1, 5)),
            dma((units + 1, 4)),
            dma((units + 1, 4)),
            dma((units + 1, 4)),
            dma((units + 1, 4)),
            dma((total // 512, 4)),
            dma((total // 512, 4)),
            dma((4,)),
            dma((4,)),
            dma((n_dp,)),
            dma((n_dp,)),
            dma((4,)),
            dma((4,)),
            dma((4,)),
            dma((5,)),
            dma((2,)),
        ],
        compiler_params=pltpu.CompilerParams(
            collective_id=1, has_side_effects=True, vmem_limit_bytes=62 * MIB
        ),
    )(
        gate1, gate2, g1, g2, dtower, tsums, pred, place, x1, x2, wa, dz2, hsy, slots
    )


def scatter_kernel(
    slots, shared, dx,
    out, bo1, bo2, bi1, bi2, gate1, gate2, tower, t_bias, t_out, t_last,
    a1, a2, a3, buf, work, raw, whole, dx_sem, out_sem,
):
    blocks, cap = slots.shape[1], slots.shape[2]
    parts = (raw, a1, a2, a3)

    def load(j):
        at = pl.ds(pl.multiple_of(j * cap, cap), cap)
        return pltpu.make_async_copy(dx.at[:, at], buf.at[j % 2], dx_sem.at[j % 2])

    load(0).start()
    for a in parts:
        a[...] = jnp.zeros_like(a)
    for q in range(4):
        for xh in range(2):
            for k in range(4):
                at = 256 * (k // 2) + 64 * q + 32 * xh + 16 * (k % 2)
                whole[at : at + 16] = shared[q, xh, k].astype(F32)
    for t in range(3):
        tower[t] = whole[128 * t : 128 * t + 128].T
    gate1[...] = jnp.concatenate([whole[384:400], whole[424:440]], axis=1).T
    gate2[...] = jnp.concatenate([whole[400:424], whole[440:464]], axis=1).T
    bo1[...] = whole[464:472]
    bo2[...] = whole[480:488]
    p = lax.axis_index("mp")
    for at, ref in ((472, bi1), (488, bi2)):
        rows = whole[at : at + 8]
        mine = jnp.zeros((8, 64), F32)
        for q in range(4):
            mine = jnp.where(p == q, rows[:, 64 * q : 64 * q + 64], mine)
        ref[...] = mine
    places = ((496, 0), (496, 128), (504, 0))
    for t, (row, lane) in enumerate(places):
        t_bias[t : t + 1] = whole[row : row + 1, lane : lane + 128]
        t_out[t : t + 1] = whole[row + 1 : row + 2, lane : lane + 128]
        t_last[:, t : t + 1] = whole[row + 2 : row + 3, lane : lane + 1]

    def block(j, carry):
        load(j).wait()

        @pl.when(j + 1 < blocks)
        def _():
            load(j + 1).start()

        wide = buf[j % 2].astype(F32)
        for q in range(4):
            work[q] = wide[q]

        def add(o, inner):
            some = work.at[:, pl.ds(pl.multiple_of(o * 8, 8), 8)]
            for u in range(8):
                for q in range(4):
                    to = pl.ds(slots[q, j, o * 8 + u], 1)
                    parts[q][to, :] += some[q, u : u + 1, :]
            return inner

        lax.fori_loop(0, cap // 8, add, 0)
        return carry

    lax.fori_loop(0, blocks, block, 0)
    rows = raw.shape[0]
    piece = rows // 4

    def store(k):
        at = pl.ds(k * piece, piece)
        return pltpu.make_async_copy(raw.at[at], out.at[at], out_sem.at[k])

    for k in range(4):
        at = slice(k * piece, (k + 1) * piece)
        raw[at] = (raw[at] + a1[at]) + (a2[at] + a3[at])
        store(k).start()
    for k in range(4):
        store(k).wait()


def scatter(slots, dx, shared, rows):
    vmem = pl.BlockSpec(memory_space=VMEM)
    hbm = pl.BlockSpec(memory_space=ANY)
    table = (rows, 128)
    cap = slots.shape[2]
    shapes = [
        table, (8, 256), (8, 256), (8, 64), (8, 64), (512, 16), (512, 24), (3, 256, 128),
        (3, 128), (3, 128), (1, 3),
    ]
    return pl.pallas_call(
        scatter_kernel,
        out_shape=[jax.ShapeDtypeStruct(shape, F32) for shape in shapes],
        in_specs=[pl.BlockSpec(memory_space=pltpu.SMEM), vmem, hbm],
        out_specs=[hbm] + [vmem] * (len(shapes) - 1),
        scratch_shapes=[
            pltpu.VMEM(table, F32),
            pltpu.VMEM(table, F32),
            pltpu.VMEM(table, F32),
            pltpu.VMEM((2, 4, cap, 128), BF16),
            pltpu.VMEM((4, cap, 128), F32),
            pltpu.VMEM(table, F32),
            pltpu.VMEM((512, 256), F32),
            pltpu.SemaphoreType.DMA((2,)),
            pltpu.SemaphoreType.DMA((4,)),
        ],
        compiler_params=pltpu.CompilerParams(vmem_limit_bytes=58 * MIB),
    )(slots, shared, dx)


def on_device(
    owner, slot, table, w_in1, b_in1, w_out1, b_out1, gate1,
    w_in2, b_in2, w_out2, b_out2, gate2,
    tower_in, tower_bias, tower_out, tower_out_bias, pred_cot,
):
    n_dp = lax.axis_size("dp")
    rows = owner.shape[0]
    cap = 4 * rows // n_dp
    g1t = gate1.reshape(gate1.shape[0], -1).T
    g2t = gate2.reshape(gate2.shape[0], -1).T
    ws1 = jnp.concatenate([w_in1.transpose(1, 2, 0), w_out1], axis=2)
    ws2 = jnp.concatenate([w_in2.transpose(1, 2, 0), w_out2], axis=2)
    small = (
        owner.reshape(1, rows), slot.reshape(1, rows), pred_cot, b_in1, b_in2, b_out1, b_out2,
        tower_bias, tower_out, tower_out_bias.reshape(1, 3), g1t, g2t, tower_in,
    )
    x1, x2, wa, hsy, dz2, slots, place, g1, g2, pred, dtower, tsums = front(
        n_dp, cap, small, ws1, ws2, table
    )
    predictions, sums, whole, dx_all, slots_all = backward(
        n_dp, g1t, g2t, g1, g2, dtower, tsums, pred, place, x1, x2, wa, dz2, hsy, slots
    )
    if n_dp == 8:
        sums = sums.reshape(2, 4, 2, 2, 2, 16, 768).transpose(0, 1, 3, 2, 4, 5, 6).astype(F32)
    else:
        sums = lax.psum(sums[:, 0].astype(F32), "dp")
        sums = sums.reshape(2, 4, 2, 2, 2, 16, 768).transpose(0, 1, 3, 2, 4, 5, 6)
        whole = lax.all_gather(lax.psum(whole[0].astype(F32), "dp"), "mp", axis=0)
        whole = whole.reshape(4, 2, 4, 16, 256).astype(BF16)
    sums = sums.reshape(2, 8, 64, 768)
    table_grad, bo1, bo2, bi1, bi2, dgate1, dgate2, tower, t_bias, t_out, t_last = scatter(
        slots_all, dx_all, whole, table.shape[0]
    )
    w_in = [sums[k, :, :, :512].transpose(2, 0, 1) for k in (1, 0)]
    return (
        predictions,
        table_grad,
        w_in[0],
        bi1,
        sums[1, :, :, 512:],
        bo1,
        dgate1.reshape(gate1.shape),
        w_in[1],
        bi2,
        sums[0, :, :, 512:],
        bo2,
        dgate2.reshape(gate2.shape),
        tower,
        t_bias,
        t_out,
        t_last.reshape(3),
    )


def solution(mesh):
    in_specs = (
        P(("dp", "mp"), None),
        P(("dp", "mp")),
        P("dp", None),
        P(None, None, "mp"),
        P(None, "mp"),
        P(None, "mp", None),
        P(),
        P(),
        P(None, None, "mp"),
        P(None, "mp"),
        P(None, "mp", None),
        P(),
        P(),
        P(),
        P(),
        P(),
        P(),
        P(None, ("dp", "mp")),
    )
    out_specs = (
        P(None, ("dp", "mp")),
        P("dp", "mp"),
        P(None, None, "mp"),
        P(None, "mp"),
        P(None, "mp", None),
        P(),
        P(),
        P(None, None, "mp"),
        P(None, "mp"),
        P(None, "mp", None),
        P(),
        P(),
        P(),
        P(),
        P(),
        P(),
    )
    return jax.shard_map(
        on_device, mesh=mesh, in_specs=in_specs, out_specs=out_specs, check_vma=False
    )
```
